32 devices in a mesh: groups: 2 (over x), slot: 16 (over z, y, core).
Axes of the slice: x: 2, y: 2, z: 4, core: 2. Of those that a mesh axis runs over, the one named last changes fastest.
Arguments:
- timesteps: int32 [32], P(('groups', 'slot')), parts along dimension 0, may hold values from 50 to 799
- prompt_ids: int32 [154], P('groups'), parts along dimension 0, may hold values from 0 to 49407
- start_latent: float32 [8, 4, 2, 128], P('groups'), parts along dimension 0, may hold values from -6 to 6
- iterate: float32 [32, 4, 4, 2, 128], P(('groups', 'slot')), parts along dimension 0, may hold values from -6 to 6
- fresh_noise: float32 [32, 4, 4, 2, 128], P(('groups', 'slot')), parts along dimension 0, may hold values from -6 to 6
- token_table: bfloat16 [49408, 1024], P('slot'), may hold values from -6 to 6
- empty_text: float32 [1024], replicated, may hold values from -6 to 6
- time_in: bfloat16 [320, 1280], replicated, may hold values from -0.3125 to 0.3125
- time_out: bfloat16 [1280, 320], replicated, may hold values from -0.15625 to 0.15625
- text_proj: bfloat16 [1024, 320], replicated, may hold values from -0.1875 to 0.1875
- conv_first: bfloat16 [9, 320, 4], replicated, may hold values from -1 to 1
- spatial_weights: bfloat16 [2, 9, 320, 320], replicated, may hold values from -0.109375 to 0.109375
- temporal_weights: bfloat16 [2, 3, 320, 320], replicated, may hold values from -0.1875 to 0.1875
- conv_last: bfloat16 [9, 4, 320], replicated, may hold values from -0.109375 to 0.109375
Outputs:
- new_iterate: float32 [32, 4, 4, 2, 128], P(('groups', 'slot')), parts along dimension 0
- final_latent: float32 [8, 4, 2, 128], P('groups'), parts along dimension 0
The draws below stay inside these ranges and needn't reach their ends.
There are 2 independent parts, one for each index of `groups`. The reference program is written for one: setup_inputs(seed, part) draws one part's arguments, and reference() takes and returns one part's arrays. A program takes and returns all parts, laid end to end along the dimension named above; an argument that names none is the same for every part. Nothing has to cross between parts.
All inputs are finite; a program needn't handle non-finite values.
Results may differ from the reference program's by a relative error of at most 0.012.
Values sent between devices are 32-bit elements; how exact they have to be, the bound alone decides.
A program may use at most 64 MiB of HBM per device.

```python
import math
import jax
import jax.numpy as jnp
import numpy as np
from jax import lax

LAT = 4
CH = 320
TIME = 1280
TEXT = 1024
VOCAB = 49408
PROMPT = 77
GROUPS = 32
SECTIONS = 2
FRAMES = 4
ROWS = 2
COLS = 128
DT = 50
TMAX = 800
SLOTS = 16


def plant(values, own_key, smallest, top_value):
    shape = values.shape
    place = [jax.random.randint(jax.random.fold_in(own_key, axis), (), 0, shape[axis]) for axis in range(len(shape))]
    values = values.at[tuple(place)].set(smallest)
    longest = shape.index(max(shape))
    place[longest] = (place[longest] + 1) % shape[longest]
    return values.at[tuple(place)].set(top_value)


def shard_levels(own_key, extent, shards, least, largest):
    def one(position, blocks):
        draws = jax.random.uniform(jax.random.fold_in(jax.random.fold_in(own_key, 6), position), (blocks,), jnp.float32, least / len(shards), largest / len(shards))
        return jnp.repeat(jnp.exp(draws), extent[position] // blocks).reshape((-1,) + (1,) * (len(extent) - position - 1))

    factor_of = one(*shards[0])
    for cut in shards[1:]:
        factor_of = factor_of * one(*cut)
    return factor_of


def rank_table(count, skew):
    weights = [(1 << 20) // math.isqrt(grade ** skew) + 1 for grade in range(1, count + 1)]
    scale = 1 + sum(weights) // (1 << 30)
    return np.cumsum(np.array([max(1, weight // scale) for weight in weights]))


def ranked_ids(own_key, shape, amount, slope):
    table = rank_table(amount, slope)
    lot = jax.random.randint(jax.random.fold_in(own_key, 1), shape, 0, int(table[amount - 1]))
    grade = jnp.searchsorted(jnp.asarray(table, jnp.int32), lot, side="right")
    return jax.random.permutation(jax.random.fold_in(own_key, 2), amount)[grade].astype(jnp.int32)


def noise(key, shape, scale, bound, split=(), kind=jnp.bfloat16):
    level = shard_levels(key, shape, split, -0.22, 0.18) if split else 1.0
    array = jax.random.normal(key, shape, jnp.float32) * scale * level
    return jnp.minimum(jnp.maximum(array, -bound), bound).astype(kind)


def setup_inputs(seed: int = 0, part: int = 0) -> dict:
    key_of = jax.random.split(jax.random.key(seed), 15)
    own_keys = jax.random.split(jax.random.fold_in(key_of[14], part), 15)
    return {
        "timesteps": plant(jax.random.randint(own_keys[0], (SLOTS,), DT, TMAX), jax.random.fold_in(own_keys[0], 1), DT, TMAX - 1).astype(jnp.int32),
        "prompt_ids": plant(ranked_ids(own_keys[1], (PROMPT,), VOCAB, 2), jax.random.fold_in(own_keys[1], 3), 0, VOCAB - 1).astype(jnp.int32),
        "start_latent": noise(own_keys[2], (LAT, FRAMES, ROWS, COLS), 1.0, 6.0, (), jnp.float32),
        "iterate": noise(own_keys[3], (SLOTS, LAT, FRAMES, ROWS, COLS), 1.0, 6.0, ((0, 16),), jnp.float32),
        "fresh_noise": noise(own_keys[4], (SLOTS, LAT, FRAMES, ROWS, COLS), 1.0, 6.0, ((0, 16),), jnp.float32),
        "token_table": noise(key_of[5], (VOCAB, TEXT), 1.0, 6.0, ((0, 16),)),
        "empty_text": noise(key_of[6], (TEXT,), 1.0, 6.0, (), jnp.float32),
        "time_in": noise(key_of[7], (CH, TIME), CH ** -0.5, 0.3125),
        "time_out": noise(key_of[8], (TIME, CH), TIME ** -0.5, 0.15625),
        "text_proj": noise(key_of[9], (TEXT, CH), TEXT ** -0.5, 0.1875),
        "conv_first": noise(key_of[10], (9, CH, LAT), (9 * LAT) ** -0.5, 1.0),
        "spatial_weights": noise(key_of[11], (SECTIONS, 9, CH, CH), (9 * CH) ** -0.5, 0.109375),
        "temporal_weights": noise(key_of[12], (SECTIONS, 3, CH, CH), (3 * CH) ** -0.5, 0.1875),
        "conv_last": noise(key_of[13], (9, LAT, CH), (9 * CH) ** -0.5, 0.109375),
    }


NORM_EPS = 1e-05
GUIDANCE_SCALE = 5.0

def alpha_bar(step_value):
    phase_angle = (step_value / 1000.0 + 0.008) / 1.008 * (jnp.pi / 2.0)
    cosine = jnp.cos(phase_angle)
    return cosine * cosine

def layer_norm(values):
    average = jnp.mean(values)
    spread = jnp.mean((values - average) ** 2)
    return (values - average) * lax.rsqrt(spread + NORM_EPS)

def group_norm(values, axes):
    batch, channels = (values.shape[0], values.shape[1])
    shaped = values.reshape((batch, GROUPS, channels // GROUPS) + values.shape[2:])
    average = lax.optimization_barrier(jnp.mean(shaped, axis=axes, keepdims=True))
    spread = lax.optimization_barrier(jnp.mean((shaped - average) ** 2, axis=axes, keepdims=True))
    return ((shaped - average) * lax.rsqrt(spread + NORM_EPS)).reshape(values.shape)

def conv_space(inputs, weight):
    padded = jnp.pad(inputs.astype(jnp.float32), ((0, 0), (0, 0), (0, 0), (1, 1), (1, 1)))
    row_count, col_count = (inputs.shape[3], inputs.shape[4])
    result = None
    for tap_index in range(9):
        row_step = tap_index // 3
        col_step = tap_index % 3
        window = padded[:, :, :, row_step:row_step + row_count, col_step:col_step + col_count]
        term = jnp.einsum('oc,bcfrw->bofrw', weight[tap_index].astype(jnp.float32), window)
        result = term if result is None else result + term
    return result

def conv_time(inputs, weight):
    padded = jnp.pad(inputs.astype(jnp.float32), ((0, 0), (0, 0), (1, 1), (0, 0), (0, 0)))
    frame_count = inputs.shape[2]
    result = None
    for tap_index in range(3):
        window = padded[:, :, tap_index:tap_index + frame_count]
        term = jnp.einsum('oc,bcfrw->bofrw', weight[tap_index].astype(jnp.float32), window)
        result = term if result is None else result + term
    return result

def reference(timesteps, prompt_ids, start_latent, iterate, fresh_noise, token_table, empty_text, time_in, time_out, text_proj, conv_first, spatial_weights, temporal_weights, conv_last):
    token_rows = token_table[prompt_ids].astype(jnp.float32)
    pooled = lax.optimization_barrier(jnp.mean(token_rows, axis=0))
    text_pair = jnp.stack([layer_norm(pooled), layer_norm(empty_text)]).astype(jnp.bfloat16)
    text_vector = jnp.dot(text_pair, text_proj, preferred_element_type=jnp.float32)
    half_width = CH // 2
    frequency = jnp.exp(-jnp.log(10000.0) * jnp.arange(half_width, dtype=jnp.float32) / half_width)

    def slot_drift(packed):
        step_index, latent, fresh = packed
        step_value = step_index.astype(jnp.float32)
        angles = step_value * frequency
        feature = jnp.concatenate([jnp.cos(angles), jnp.sin(angles)]).astype(jnp.bfloat16)[None, :]
        hidden = jax.nn.silu(jnp.dot(feature, time_in, preferred_element_type=jnp.float32)).astype(jnp.bfloat16)
        time_vector = jnp.dot(hidden, time_out, preferred_element_type=jnp.float32)
        embedding = text_vector + time_vector
        state = (conv_space(latent.astype(jnp.bfloat16)[None], conv_first) + embedding[:, :, None, None, None]).astype(jnp.bfloat16)
        for section in range(SECTIONS):
            normed = jax.nn.silu(group_norm(state.astype(jnp.float32), (2, 4, 5))).astype(jnp.bfloat16)
            state = (state.astype(jnp.float32) + conv_space(normed, spatial_weights[section])).astype(jnp.bfloat16)
            normed = jax.nn.silu(group_norm(state.astype(jnp.float32), (2, 3, 4, 5))).astype(jnp.bfloat16)
            state = (state.astype(jnp.float32) + conv_time(normed, temporal_weights[section])).astype(jnp.bfloat16)
        normed = jax.nn.silu(group_norm(state.astype(jnp.float32), (2, 4, 5))).astype(jnp.bfloat16)
        predicted = conv_space(normed, conv_last)
        guided = predicted[1] + GUIDANCE_SCALE * (predicted[0] - predicted[1])
        alpha_now = alpha_bar(step_value)
        alpha_prev = alpha_bar(step_value - DT)
        scale_ratio = jnp.sqrt(alpha_prev / alpha_now)
        noise_square = (1.0 - alpha_prev) * (1.0 - alpha_now / alpha_prev) / (1.0 - alpha_now)
        kept_square = (1.0 - alpha_prev) * (alpha_now / alpha_prev - alpha_now) / (1.0 - alpha_now)
        eps_factor = jnp.sqrt(kept_square) - scale_ratio * jnp.sqrt(1.0 - alpha_now)
        return (scale_ratio - 1.0) * latent + eps_factor * guided + jnp.sqrt(noise_square) * fresh
    drifts = lax.map(slot_drift, (timesteps, iterate, fresh_noise))
    running = jnp.cumsum(drifts, axis=0)
    earlier = jnp.concatenate([jnp.zeros_like(drifts[:1]), running[:-1]], axis=0)
    new_iterate = start_latent[None] + earlier
    final_latent = start_latent + lax.optimization_barrier(jnp.sum(drifts, axis=0))
    return (new_iterate, final_latent)
```

```python
import functools

import jax
import jax.numpy as jnp
import numpy as np
from jax import lax
from jax.experimental import pallas as pl
from jax.experimental.pallas import tpu as pltpu
from jax.sharding import PartitionSpec as P

GROUPS = 32
DT = 50
NORM_EPS = 1e-05
GUIDANCE_SCALE = 5.0
LANES = 128
PAD = 1024
F32 = jnp.float32
BF16 = jnp.bfloat16


def alpha_bar(step_value):
    phase_angle = (step_value / 1000.0 + 0.008) / 1.008 * (jnp.pi / 2.0)
    cosine = jnp.cos(phase_angle)
    return cosine * cosine


def layer_norm(values):
    average = jnp.mean(values, axis=-1, keepdims=True)
    spread = jnp.mean((values - average) ** 2, axis=-1, keepdims=True)
    return (values - average) * lax.rsqrt(spread + NORM_EPS)


def silu(values):
    half = 0.5 * values
    return half + half * jnp.tanh(half)


def dot(a, b):
    return jnp.dot(a, b, preferred_element_type=F32)


def shift(tile, step):
    if step == 0:
        return tile
    lane = lax.broadcasted_iota(jnp.int32, tile.shape, 1)
    rolled = pltpu.roll(tile, (-step) % LANES, axis=1)
    return jnp.where(lane == (LANES - 1 if step == 1 else 0), 0.0, rolled)


def group_matrix(channels):
    size = channels // GROUPS
    group = lax.broadcasted_iota(jnp.int32, (GROUPS, channels), 0) * size
    channel = lax.broadcasted_iota(jnp.int32, (GROUPS, channels), 1)
    return jnp.where((channel >= group) & (channel < group + size), 1.0, 0.0).astype(BF16)


def expand_matrix(channels):
    size = channels // GROUPS
    channel = lax.broadcasted_iota(jnp.int32, (channels, 3 * GROUPS), 0)
    group = (lax.broadcasted_iota(jnp.int32, (channels, 3 * GROUPS), 1) & (GROUPS - 1)) * size
    return jnp.where((channel >= group) & (channel < group + size), 1.0, 0.0).astype(BF16)


def spread_groups(expand, stat):
    high = stat.astype(BF16)
    rest = stat - high.astype(F32)
    middle = rest.astype(BF16)
    low = (rest - middle.astype(F32)).astype(BF16)
    return dot(expand, jnp.concatenate([high, middle, low], axis=0))


def lane_means(sums, frames, count, temporal):
    if temporal:
        folded = sum(sums[:, f * LANES : (f + 1) * LANES] for f in range(frames))
        total = jnp.sum(folded, axis=1, keepdims=True) * (1.0 / (count * frames))
        return jnp.broadcast_to(total, sums.shape)
    parts = []
    for f in range(frames):
        total = jnp.sum(sums[:, f * LANES : (f + 1) * LANES], axis=1, keepdims=True)
        parts.append(jnp.broadcast_to(total * (1.0 / count), (sums.shape[0], LANES)))
    return jnp.concatenate(parts, axis=1)


def norm_silu(state, gather, expand, frames, temporal):
    rows, channels, _ = state.shape
    count = (channels // GROUPS) * rows * LANES
    sums = sum(dot(gather, state[r]) for r in range(rows))
    mean = spread_groups(expand, lane_means(sums, frames, count, temporal))
    centred = [state[r].astype(F32) - mean for r in range(rows)]
    square = sum(c * c for c in centred)
    high = square.astype(BF16)
    low = (square - high.astype(F32)).astype(BF16)
    spread = lane_means(dot(gather, high) + dot(gather, low), frames, count, temporal)
    scale = spread_groups(expand, lax.rsqrt(spread + NORM_EPS))
    return [silu(c * scale) for c in centred]


def sample_body(step_value, emb, latent, w_first, spatial, temporal, w_last, scratch, ready):
    state, xs, xt, wcat, wt, first_in = scratch
    sections, _, channels, _ = spatial.shape
    lat, frames, rows = latent.shape[1:4]
    gather = group_matrix(channels)
    expand = expand_matrix(channels)
    three = 3 * channels

    xs[...] = jnp.zeros_like(xs)
    xt[...] = jnp.zeros_like(xt)

    first_in[...] = jnp.zeros_like(first_in)
    for r in range(rows):
        for f in range(frames):
            tile = jnp.concatenate([latent[0, l, f, pl.ds(r, 1), :] for l in range(lat)], axis=0)
            for k in range(3):
                first_in[pl.ds((r + 1) * 3 * lat + k * lat, lat), pl.ds(f * LANES, LANES)] = shift(
                    tile, k - 1
                )
    ready("first")
    weight = jnp.concatenate([w_first[k].astype(F32) for k in range(9)], axis=1).astype(BF16)
    column = jnp.broadcast_to(emb, (LANES, channels)).T
    column = jnp.concatenate([column] * frames, axis=1)
    for r in range(rows):
        window = first_in[pl.ds((r * 3) * lat, 9 * lat), :] if r else first_in[pl.ds(0, 9 * lat), :]
        state[r] = (dot(weight, window.astype(BF16)) + column).astype(BF16)

    blank = jnp.zeros((channels, PAD - three), BF16)
    for s in range(sections):
        ready("spatial", s)
        for g in range(3):
            wcat[:, pl.ds(g * PAD, PAD)] = jnp.concatenate(
                [spatial[s, 3 * g + k] for k in range(3)] + [blank], axis=1
            )
        normed = norm_silu(state[...], gather, expand, frames, False)
        for r in range(rows):
            for f in range(frames):
                at = pl.ds(f * LANES, LANES)
                tile = normed[r][:, f * LANES : (f + 1) * LANES]
                for k in range(3):
                    xs[pl.ds(r * PAD + k * channels, channels), at] = shift(tile, k - 1).astype(BF16)
        for r in range(rows):
            moved = dot(wcat[:, pl.ds((1 - r) * PAD, 2 * PAD)], xs[...])
            state[r] = (state[r].astype(F32) + moved).astype(BF16)
        ready("temporal", s)
        wt[...] = jnp.concatenate([temporal[s, k] for k in range(3)] + [blank], axis=1)
        normed = norm_silu(state[...], gather, expand, frames, True)
        for r in range(rows):
            for f in range(frames):
                tile = normed[r][:, f * LANES : (f + 1) * LANES].astype(BF16)
                for k in range(3):
                    to = f - (k - 1)
                    if 0 <= to < frames:
                        xt[pl.ds(k * channels, channels), pl.ds((r * frames + to) * LANES, LANES)] = tile
        for r in range(rows):
            moved = dot(wt[...], xt[:, pl.ds(r * frames * LANES, frames * LANES)])
            state[r] = (state[r].astype(F32) + moved).astype(BF16)

    normed = norm_silu(state[...], gather, expand, frames, False)
    ready("last")
    taps = [dot(w_last[...], normed[r].astype(BF16)) for r in range(rows)]
    predicted = []
    for r in range(rows):
        per_frame = []
        for f in range(frames):
            total = None
            for k in range(3):
                tile = sum(
                    taps[q][((q - r + 1) * 3 + k) * lat :][:lat, f * LANES : (f + 1) * LANES]
                    for q in range(rows)
                )
                term = shift(tile, k - 1)
                total = term if total is None else total + term
            per_frame.append(total)
        predicted.append(per_frame)
    return predicted


def step_of(timesteps):
    return jnp.full((8, LANES), timesteps[0], jnp.int32).astype(F32)


def text_row(row, text_proj):
    pair = layer_norm(row).astype(BF16)
    return dot(jnp.broadcast_to(pair, (16, row.shape[1])), text_proj[...])[0:1]


def loader(sem, names):
    copies = {}
    for index, (key, source, target) in enumerate(names):
        copies[key] = pltpu.make_async_copy(source, target, sem.at[index])
    for copy in copies.values():
        copy.start()

    def ready(*key):
        copies[key].wait()

    return ready


def weight_copies(first_hbm, spatial_hbm, temporal_hbm, last_hbm, first, spatial, temporal, last):
    names = [(("first",), first_hbm, first)]
    for s in range(spatial_hbm.shape[0]):
        names.append((("spatial", s), spatial_hbm.at[s], spatial.at[s]))
        names.append((("temporal", s), temporal_hbm.at[s], temporal.at[s]))
    names.append((("last",), last_hbm, last))
    return names


def uncond_kernel(
    timesteps, empty, latent, time_in_hbm, time_out_hbm, text_hbm, first_hbm, spatial_hbm,
    temporal_hbm, last_hbm, pred_out, tvec_out,
    time_in, time_out, text_proj, first, spatial, temporal, last, sem, *scratch
):
    names = [
        (("time_in",), time_in_hbm, time_in),
        (("time_out",), time_out_hbm, time_out),
        (("text",), text_hbm, text_proj),
    ]
    names += weight_copies(
        first_hbm, spatial_hbm, temporal_hbm, last_hbm, first, spatial, temporal, last
    )
    ready = loader(sem, names)
    channels = time_in.shape[0]
    half = channels // 2
    lane = lax.broadcasted_iota(jnp.int32, (16, channels), 1)
    place = jnp.where(lane < half, lane, lane - half).astype(F32)
    step = jnp.full((16, channels), timesteps[0], jnp.int32).astype(F32)
    angles = step * jnp.exp(np.float32(-np.log(10000.0)) * place / half)
    feature = jnp.where(lane < half, jnp.cos(angles), jnp.sin(angles)).astype(BF16)
    ready("time_in")
    hidden = silu(dot(feature, time_in[...])).astype(BF16)
    ready("time_out")
    tvec = dot(hidden, time_out[...])[0:1]
    tvec_out[...] = tvec
    ready("text")
    emb = tvec + text_row(empty[...], text_proj)
    predicted = sample_body(None, emb, latent, first, spatial, temporal, last, scratch, ready)
    for r, per_frame in enumerate(predicted):
        for f, tile in enumerate(per_frame):
            pred_out[r, f] = tile


def cond_kernel(
    prompt, timesteps, pooled, tvec, latent, fresh, uncond, text_hbm, first_hbm, spatial_hbm,
    temporal_hbm, last_hbm, drift_out,
    text_proj, first, spatial, temporal, last, sem, *scratch
):
    names = [(("text",), text_hbm, text_proj)]
    names += weight_copies(
        first_hbm, spatial_hbm, temporal_hbm, last_hbm, first, spatial, temporal, last
    )
    ready = loader(sem, names)
    ready("text")
    emb = tvec[...] + text_row(pooled[...] * (1.0 / prompt), text_proj)
    predicted = sample_body(None, emb, latent, first, spatial, temporal, last, scratch, ready)
    step_value = step_of(timesteps)
    now = alpha_bar(step_value)
    prev = alpha_bar(step_value - DT)
    ratio = jnp.sqrt(prev / now)
    noise_square = (1.0 - prev) * (1.0 - now / prev) / (1.0 - now)
    kept_square = (1.0 - prev) * (now / prev - now) / (1.0 - now)
    eps_factor = (jnp.sqrt(kept_square) - ratio * jnp.sqrt(1.0 - now))[0:1]
    noise_factor = jnp.sqrt(noise_square)[0:1]
    keep = (ratio - 1.0)[0:1]
    lat = latent.shape[1]
    for r, per_frame in enumerate(predicted):
        for f, tile in enumerate(per_frame):
            without = uncond[r, f]
            guided = without + GUIDANCE_SCALE * (tile - without)
            for l in range(lat):
                drift_out[l, f, pl.ds(r, 1), :] = (
                    keep * latent[0, l, f, pl.ds(r, 1), :]
                    + eps_factor * guided[l : l + 1]
                    + noise_factor * fresh[0, l, f, pl.ds(r, 1), :]
                )


def exchange_kernel(
    n, drift, start, new_out, final_out, inbox, result, outbox, send1, recv1, send2, recv2, lsem
):
    pieces = drift.shape[0]
    stride = n // pieces
    me = lax.axis_index("slot")
    mine = me // stride
    owner = lax.rem(me, stride) == 0
    barrier = pltpu.get_barrier_semaphore()

    def to(slot):
        return {"slot": slot}

    for k in range(1, n):
        pl.semaphore_signal(
            barrier, inc=1, device_id=to(lax.rem(me + k, n)), device_id_type=pl.DeviceIdType.MESH
        )
    pl.semaphore_wait(barrier, n - 1)

    def first_copy(k):
        piece = lax.rem(mine + k, pieces)
        return pltpu.make_async_remote_copy(
            src_ref=drift.at[piece], dst_ref=inbox.at[me], send_sem=send1.at[k],
            recv_sem=recv1.at[me], device_id=to(piece * stride),
            device_id_type=pl.DeviceIdType.MESH,
        )

    def second_copy(k):
        slot = lax.rem(me + k, n)
        return pltpu.make_async_remote_copy(
            src_ref=result.at[slot], dst_ref=outbox.at[mine], send_sem=send2.at[k],
            recv_sem=recv2.at[mine], device_id=to(slot), device_id_type=pl.DeviceIdType.MESH,
        )

    for k in range(1, pieces):
        first_copy(k).start()

    if stride > 1:
        @pl.when(jnp.logical_not(owner))
        def _():
            first_copy(0).start()

    @pl.when(owner)
    def _():
        inbox[me] = drift[mine]
        for k in range(1, n):
            slot = lax.rem(me + k, n)
            pltpu.make_async_remote_copy(
                src_ref=drift.at[mine], dst_ref=inbox.at[slot], send_sem=send1.at[0],
                recv_sem=recv1.at[slot], device_id=to(slot), device_id_type=pl.DeviceIdType.MESH,
            ).wait_recv()
        running = start[mine]
        for j in range(n):
            result[j, 0] = running
            running = running + inbox[j]
        for j in range(n):
            result[j, 1] = running
        for k in range(1, n):
            second_copy(k).start()
        outbox[mine] = result[me]

    for k in range(1, pieces):
        piece = lax.rem(mine + k, pieces)
        pltpu.make_async_remote_copy(
            src_ref=result.at[0], dst_ref=outbox.at[piece], send_sem=send2.at[0],
            recv_sem=recv2.at[piece], device_id=to(piece * stride),
            device_id_type=pl.DeviceIdType.MESH,
        ).wait_recv()
    if stride > 1:
        @pl.when(jnp.logical_not(owner))
        def _():
            pltpu.make_async_remote_copy(
                src_ref=result.at[0], dst_ref=outbox.at[mine], send_sem=send2.at[0],
                recv_sem=recv2.at[mine], device_id=to(mine * stride),
                device_id_type=pl.DeviceIdType.MESH,
            ).wait_recv()
            first_copy(0).wait_send()
    new_out[...] = outbox[:, 0]
    final_out[...] = outbox[:, 1]
    for k in range(1, pieces):
        first_copy(k).wait_send()

    @pl.when(owner)
    def _():
        for k in range(1, n):
            second_copy(k).wait_send()


VMEM = pl.BlockSpec(memory_space=pltpu.VMEM)
SMEM = pl.BlockSpec(memory_space=pltpu.SMEM)
ANY = pl.BlockSpec(memory_space=pl.ANY)


def like(array):
    return pltpu.VMEM(array.shape, array.dtype)


def local(
    timesteps, prompt_ids, start_latent, iterate, fresh_noise, token_table, empty_text, time_in,
    time_out, text_proj, conv_first, spatial_weights, temporal_weights, conv_last,
):
    n = lax.axis_size("slot")
    shard_rows = token_table.shape[0]
    local_ids = prompt_ids - lax.axis_index("slot") * shard_rows
    counts = jnp.sum(
        (local_ids[:, None] == jnp.arange(shard_rows, dtype=jnp.int32)[None, :]).astype(F32),
        axis=0, keepdims=True,
    ).astype(BF16)
    partial_sum = jnp.dot(counts, token_table, preferred_element_type=F32)
    pooled = lax.psum(partial_sum, "slot")

    lat, frames, rows, cols = iterate.shape[1:]
    sections, _, channels, _ = spatial_weights.shape
    last = conv_last.reshape(9 * lat, channels)
    width = frames * cols
    scratch = [
        pltpu.VMEM((rows, channels, width), BF16),
        pltpu.VMEM((rows * PAD, width), BF16),
        pltpu.VMEM((PAD, rows * width), BF16),
        pltpu.VMEM((channels, 3 * PAD), BF16),
        pltpu.VMEM((channels, PAD), BF16),
        pltpu.VMEM((12 * lat, width), F32),
    ]
    weights = [conv_first, spatial_weights, temporal_weights, last]
    count = 2 + 2 * sections
    cost = pl.CostEstimate(flops=4_000_000_000, bytes_accessed=7_000_000, transcendentals=1_600_000)
    params = pltpu.CompilerParams(vmem_limit_bytes=48 * 1024 * 1024)
    uncond, tvec = pl.pallas_call(
        uncond_kernel,
        out_shape=(
            jax.ShapeDtypeStruct((rows, frames, lat, cols), F32),
            jax.ShapeDtypeStruct((1, channels), F32),
        ),
        in_specs=[SMEM, VMEM, VMEM] + [ANY] * 7,
        out_specs=(VMEM, VMEM),
        scratch_shapes=[like(time_in), like(time_out), like(text_proj)]
        + [like(w) for w in weights]
        + [pltpu.SemaphoreType.DMA((3 + count,))]
        + scratch,
        compiler_params=params,
        cost_estimate=cost,
        name="uncond_sample",
    )(timesteps, empty_text[None], iterate, time_in, time_out, text_proj, *weights)
    drift = pl.pallas_call(
        functools.partial(cond_kernel, prompt_ids.shape[0]),
        out_shape=jax.ShapeDtypeStruct((lat, frames, rows, cols), F32),
        in_specs=[SMEM] + [VMEM] * 5 + [ANY] * 5,
        out_specs=VMEM,
        scratch_shapes=[like(text_proj)]
        + [like(w) for w in weights]
        + [pltpu.SemaphoreType.DMA((1 + count,))]
        + scratch,
        compiler_params=params,
        cost_estimate=cost,
        name="cond_sample",
    )(timesteps, pooled, tvec, iterate, fresh_noise, uncond, text_proj, *weights)

    pieces = lat * frames
    piece = (rows, cols)
    shape = jax.ShapeDtypeStruct((pieces,) + piece, F32)
    new, final = pl.pallas_call(
        functools.partial(exchange_kernel, n),
        out_shape=(shape, shape),
        in_specs=[VMEM, VMEM],
        out_specs=(VMEM, VMEM),
        scratch_shapes=[
            pltpu.VMEM((n,) + piece, F32),
            pltpu.VMEM((n, 2) + piece, F32),
            pltpu.VMEM((pieces, 2) + piece, F32),
            pltpu.SemaphoreType.DMA((pieces,)),
            pltpu.SemaphoreType.DMA((n,)),
            pltpu.SemaphoreType.DMA((n,)),
            pltpu.SemaphoreType.DMA((pieces,)),
            pltpu.SemaphoreType.DMA,
        ],
        compiler_params=pltpu.CompilerParams(collective_id=0, has_side_effects=True),
        name="exchange",
    )(drift.reshape(shape.shape), start_latent.reshape(shape.shape))
    return new.reshape(iterate.shape), final.reshape(start_latent.shape)


def solution(mesh):
    placed = (
        P(("groups", "slot")),
        P("groups"),
        P("groups", None, None, None),
        P(("groups", "slot"), None, None, None, None),
        P(("groups", "slot"), None, None, None, None),
        P("slot", None),
    ) + (P(),) * 8
    return jax.shard_map(
        local,
        mesh=mesh,
        in_specs=placed,
        out_specs=(P(("groups", "slot"), None, None, None, None), P("groups", None, None, None)),
        check_vma=False,
    )
```

```python
import functools

import jax
import jax.numpy as jnp
import numpy as np
from jax import lax
from jax.experimental import pallas as pl
from jax.experimental.pallas import tpu as pltpu
from jax.sharding import PartitionSpec as P

GROUPS = 32
DT = 50
NORM_EPS = 1e-05
GUIDANCE_SCALE = 5.0
LANES = 128
PAD = 1024
F32 = jnp.float32
BF16 = jnp.bfloat16
LEAD = 3


def alpha_bar(step_value):
    phase_angle = (step_value / 1000.0 + 0.008) / 1.008 * (jnp.pi / 2.0)
    cosine = jnp.cos(phase_angle)
    return cosine * cosine


def layer_norm(values):
    average = jnp.mean(values, axis=-1, keepdims=True)
    spread = jnp.mean((values - average) ** 2, axis=-1, keepdims=True)
    return (values - average) * lax.rsqrt(spread + NORM_EPS)


def silu(values):
    half = 0.5 * values
    return half + half * jnp.tanh(half)


def dot(a, b):
    return jnp.dot(a, b, preferred_element_type=F32)


def shift(tile, step):
    if step == 0:
        return tile
    lane = lax.broadcasted_iota(jnp.int32, tile.shape, 1)
    rolled = pltpu.roll(tile, (-step) % LANES, axis=1)
    return jnp.where(lane == (LANES - 1 if step == 1 else 0), 0.0, rolled)


def group_matrix(channels):
    size = channels // GROUPS
    group = lax.broadcasted_iota(jnp.int32, (GROUPS, channels), 0) * size
    channel = lax.broadcasted_iota(jnp.int32, (GROUPS, channels), 1)
    return jnp.where((channel >= group) & (channel < group + size), 1.0, 0.0).astype(BF16)


def expand_matrix(channels):
    size = channels // GROUPS
    channel = lax.broadcasted_iota(jnp.int32, (channels, 3 * GROUPS), 0)
    group = (lax.broadcasted_iota(jnp.int32, (channels, 3 * GROUPS), 1) & (GROUPS - 1)) * size
    return jnp.where((channel >= group) & (channel < group + size), 1.0, 0.0).astype(BF16)


def spread_groups(expand, stat):
    high = stat.astype(BF16)
    rest = stat - high.astype(F32)
    middle = rest.astype(BF16)
    low = (rest - middle.astype(F32)).astype(BF16)
    return dot(expand, jnp.concatenate([high, middle, low], axis=0))


def lane_means(sums, frames, count, temporal):
    if temporal:
        folded = sum(sums[:, f * LANES : (f + 1) * LANES] for f in range(frames))
        total = jnp.sum(folded, axis=1, keepdims=True) * (1.0 / (count * frames))
        return jnp.broadcast_to(total, sums.shape)
    parts = []
    for f in range(frames):
        total = jnp.sum(sums[:, f * LANES : (f + 1) * LANES], axis=1, keepdims=True)
        parts.append(jnp.broadcast_to(total * (1.0 / count), (sums.shape[0], LANES)))
    return jnp.concatenate(parts, axis=1)


def norm_silu(state, gather, expand, frames, temporal):
    rows, channels, _ = state.shape
    count = (channels // GROUPS) * rows * LANES
    sums = sum(dot(gather, state[r]) for r in range(rows))
    mean = spread_groups(expand, lane_means(sums, frames, count, temporal))
    centred = [state[r].astype(F32) - mean for r in range(rows)]
    square = sum(c * c for c in centred)
    high = square.astype(BF16)
    low = (square - high.astype(F32)).astype(BF16)
    spread = lane_means(dot(gather, high) + dot(gather, low), frames, count, temporal)
    scale = spread_groups(expand, lax.rsqrt(spread + NORM_EPS))
    return [silu(c * scale) for c in centred]


def dot_nt(a, b):
    return lax.dot_general(a, b, (((1,), (1,)), ((), ())), preferred_element_type=F32)


def small_taps(weight, rows):
    taps = [weight[k].astype(F32) for k in range(9)]
    lat, channels = taps[0].shape
    return jnp.concatenate(taps + [jnp.zeros((rows - 9 * lat, channels), F32)], axis=0)


def first_windows(latent, first_in):
    lat, frames, rows = latent.shape[1:4]
    first_in[...] = jnp.zeros_like(first_in)
    for r in range(rows):
        for f in range(frames):
            tile = jnp.concatenate([latent[0, l, f, pl.ds(r, 1), :] for l in range(lat)], axis=0)
            for k in range(3):
                first_in[pl.ds((r + 1) * 3 * lat + k * lat, lat), pl.ds(f * LANES, LANES)] = shift(
                    tile, k - 1
                )


def sample_steps(emb, weight, first_in, wcat, wt, w_last, scratch, consts, sizes, predicted, ready):
    state, xs, xt = scratch
    gather, expand = consts
    sections, channels, lat, frames, rows = sizes
    column = jnp.broadcast_to(emb, (LANES, channels)).T
    column = jnp.concatenate([column] * frames, axis=1)
    for r in range(rows):
        window = first_in[pl.ds(r * 3 * lat, weight.shape[1]), :].astype(BF16)
        state[r] = (dot(weight, window) + column).astype(BF16)
    yield
    for s in range(sections):
        normed = norm_silu(state[...], gather, expand, frames, False)
        for r in range(rows):
            for f in range(frames):
                at = pl.ds(f * LANES, LANES)
                tile = normed[r][:, f * LANES : (f + 1) * LANES]
                for k in range(3):
                    xs[pl.ds(r * PAD + k * channels, channels), at] = shift(tile, k - 1).astype(BF16)
        yield
        ready("spatial", s)
        for r in range(rows):
            moved = dot(wcat[s, :, pl.ds((1 - r) * PAD, 2 * PAD)], xs[...])
            state[r] = (state[r].astype(F32) + moved).astype(BF16)
        yield
        normed = norm_silu(state[...], gather, expand, frames, True)
        for r in range(rows):
            for f in range(frames):
                tile = normed[r][:, f * LANES : (f + 1) * LANES].astype(BF16)
                for k in range(3):
                    to = f - (k - 1)
                    if 0 <= to < frames:
                        xt[pl.ds(k * channels, channels), pl.ds((r * frames + to) * LANES, LANES)] = tile
        yield
        ready("temporal", s)
        for r in range(rows):
            moved = dot(wt[s], xt[:, pl.ds(r * frames * LANES, frames * LANES)])
            state[r] = (state[r].astype(F32) + moved).astype(BF16)
        yield
    normed = norm_silu(state[...], gather, expand, frames, False)
    yield
    ready("last")
    taps_last = small_taps(w_last, 48).astype(BF16)
    taps = [dot(taps_last, normed[r].astype(BF16)) for r in range(rows)]
    for r in range(rows):
        for f in range(frames):
            total = None
            for k in range(3):
                tile = sum(
                    taps[q][((q - r + 1) * 3 + k) * lat :][:lat, f * LANES : (f + 1) * LANES]
                    for q in range(rows)
                )
                term = shift(tile, k - 1)
                total = term if total is None else total + term
            predicted[r][f] = total
    yield


def text_row(row, text_proj):
    pair = layer_norm(row).astype(BF16)
    return dot_nt(jnp.broadcast_to(pair, (16, row.shape[1])), text_proj[...])[0:1]


def time_row(timesteps, time_in, time_out, ready):
    channels = time_in.shape[0]
    half = channels // 2
    lane = lax.broadcasted_iota(jnp.int32, (16, channels), 1)
    place = jnp.where(lane < half, lane, lane - half).astype(F32)
    step = jnp.full((16, channels), timesteps[0], jnp.int32).astype(F32)
    angles = step * jnp.exp(np.float32(-np.log(10000.0)) * place / half)
    feature = jnp.where(lane < half, jnp.cos(angles), jnp.sin(angles)).astype(BF16)
    ready("time_in")
    hidden = silu(dot(feature, time_in[...])).astype(BF16)
    ready("time_out")
    return dot_nt(hidden, time_out[...])[0:1]


def drift_factors(timesteps):
    step_value = jnp.full((8, LANES), timesteps[0], jnp.int32).astype(F32)
    now = alpha_bar(step_value)
    prev = alpha_bar(step_value - DT)
    ratio = jnp.sqrt(prev / now)
    noise_square = (1.0 - prev) * (1.0 - now / prev) / (1.0 - now)
    kept_square = (1.0 - prev) * (now / prev - now) / (1.0 - now)
    eps_factor = (jnp.sqrt(kept_square) - ratio * jnp.sqrt(1.0 - now))[0:1]
    return (ratio - 1.0)[0:1], eps_factor, jnp.sqrt(noise_square)[0:1]


def token_counts(prompt, shard_rows, me):
    amount = prompt.shape[0]
    base = me * shard_rows
    sub = lax.broadcasted_iota(jnp.int32, (16, LANES), 0)
    wide = -(-shard_rows // LANES) * LANES
    lane = lax.broadcasted_iota(jnp.int32, (16, wide), 1)
    counts = jnp.zeros((16, wide), F32)
    for start in range(0, amount, 16):
        column = jnp.full((16, LANES), -1, jnp.int32)
        for j in range(min(16, amount - start)):
            column = jnp.where(sub == j, prompt[start + j] - base, column)
        column = jnp.concatenate([column] * (wide // LANES), axis=1)
        counts = counts + jnp.where(lane == column, 1.0, 0.0)
    return counts[:, :shard_rows].astype(BF16)


def sweep_kernel(
    n, prompt, timesteps, empty, start, latent, fresh, first, last, table_hbm, time_in_hbm,
    time_out_hbm, text_hbm, spatial_hbm, temporal_hbm, result_out,
    table, time_in, time_out, text_proj, spatial, temporal, sem,
    wcat, wt, first_in, state_u, xs_u, xt_u, state_c, xs_c, xt_c,
    partial, pool, drift, inbox, result, outbox, sendp, recvp, send1, recv1, send2, recv2,
):
    mesh_id = pl.DeviceIdType.MESH
    sections, _, channels, _ = spatial.shape
    lat, frames, rows = latent.shape[1:4]
    me = lax.axis_index("slot")
    barrier = pltpu.get_barrier_semaphore()

    def to(slot):
        return {"slot": slot}

    copies = {}
    names = [
        (("time_in",), time_in_hbm, time_in),
        (("time_out",), time_out_hbm, time_out),
        (("text",), text_hbm, text_proj),
        (("table",), table_hbm, table),
    ]
    for s in range(sections):
        names.append((("spatial", s), spatial_hbm.at[s], spatial.at[s]))
        names.append((("temporal", s), temporal_hbm.at[s], temporal.at[s]))
    for index, (key, source, target) in enumerate(names):
        copies[key] = pltpu.make_async_copy(source, target, sem.at[index])
        copies[key].start()
    for k in range(1, n):
        pl.semaphore_signal(barrier, inc=1, device_id=to(lax.rem(me + k, n)), device_id_type=mesh_id)

    done = set()
    blank = jnp.zeros((channels, PAD - 3 * channels), BF16)

    def ready(*key):
        if key in done:
            return
        done.add(key)
        if key in copies:
            copies[key].wait()
        if key[0] == "spatial":
            s = key[1]
            for g in range(3):
                wcat[s, :, pl.ds(g * PAD, PAD)] = jnp.concatenate(
                    [spatial[s, 3 * g + k] for k in range(3)] + [blank], axis=1
                )
        if key[0] == "temporal":
            s = key[1]
            wt[s] = jnp.concatenate([temporal[s, k] for k in range(3)] + [blank], axis=1)

    for ref in (xs_u, xs_c):
        for r in range(rows):
            ref[pl.ds(r * PAD + 3 * channels, PAD - 3 * channels), :] = jnp.zeros(
                (PAD - 3 * channels, ref.shape[1]), BF16
            )
    for ref in (xt_u, xt_c):
        ref[...] = jnp.zeros_like(ref)
    counts = token_counts(prompt, table.shape[0], me)
    first_windows(latent, first_in)
    weight = small_taps(first, 40).T.astype(BF16)
    consts = (group_matrix(channels), expand_matrix(channels))
    sizes = (sections, channels, lat, frames, rows)
    keep, eps_factor, noise_factor = drift_factors(timesteps)
    tvec = time_row(timesteps, time_in, time_out, ready)
    ready("text")
    emb_u = tvec + text_row(empty[...], text_proj)

    ready("table")
    partial[...] = jnp.sum(dot(counts, table[...]), axis=0, keepdims=True)
    pl.semaphore_wait(barrier, n - 1)

    def pooled_copy(k):
        return pltpu.make_async_remote_copy(
            src_ref=partial, dst_ref=pool.at[me], send_sem=sendp.at[k], recv_sem=recvp.at[me],
            device_id=to(lax.rem(me + k, n)), device_id_type=mesh_id,
        )

    for k in range(1, n):
        pooled_copy(k).start()
    pool[me] = partial[...]

    pred_u = [[None] * frames for _ in range(rows)]
    pred_c = [[None] * frames for _ in range(rows)]
    steps_u = sample_steps(
        emb_u, weight, first_in, wcat, wt, last, (state_u, xs_u, xt_u), consts, sizes, pred_u, ready
    )
    for _ in range(LEAD):
        next(steps_u)

    for s in range(sections):
        ready("spatial", s)
        ready("temporal", s)
    for k in range(1, n):
        slot = lax.rem(me + k, n)
        pltpu.make_async_remote_copy(
            src_ref=partial, dst_ref=pool.at[slot], send_sem=sendp.at[0], recv_sem=recvp.at[slot],
            device_id=to(slot), device_id_type=mesh_id,
        ).wait_recv()
    pooled = pool[0]
    for k in range(1, n):
        pooled = pooled + pool[k]
    emb_c = tvec + text_row(pooled * (1.0 / prompt.shape[0]), text_proj)
    steps_c = sample_steps(
        emb_c, weight, first_in, wcat, wt, last, (state_c, xs_c, xt_c), consts, sizes, pred_c, ready
    )
    live = True
    while live:
        live = next(steps_c, 0) is None
        next(steps_u, 0)

    for r in range(rows):
        for f in range(frames):
            without = pred_u[r][f]
            guided = without + GUIDANCE_SCALE * (pred_c[r][f] - without)
            for l in range(lat):
                drift[l * frames + f, pl.ds(r, 1), :] = (
                    keep * latent[0, l, f, pl.ds(r, 1), :]
                    + eps_factor * guided[l : l + 1]
                    + noise_factor * fresh[0, l, f, pl.ds(r, 1), :]
                )
    exchange(
        n, me, to, drift, start, result_out, inbox, result, outbox, send1, recv1, send2, recv2
    )
    for k in range(1, n):
        pooled_copy(k).wait_send()


def exchange(
    n, me, to, drift, start, result_out, inbox, result, outbox, send1, recv1, send2, recv2
):
    pieces = drift.shape[0]
    stride = n // pieces
    mine = me // stride if stride > 1 else me
    mesh_id = pl.DeviceIdType.MESH

    def for_owner(body):
        pl.when(lax.rem(me, stride) == 0)(body) if stride > 1 else body()

    def for_others(body):
        if stride > 1:
            pl.when(lax.rem(me, stride) != 0)(body)

    def first_copy(k):
        piece = lax.rem(mine + k, pieces)
        return pltpu.make_async_remote_copy(
            src_ref=drift.at[piece], dst_ref=inbox.at[me], send_sem=send1.at[k],
            recv_sem=recv1.at[me], device_id=to(piece * stride), device_id_type=mesh_id,
        )

    def second_copy(k):
        slot = lax.rem(me + k, n)
        return pltpu.make_async_remote_copy(
            src_ref=result.at[slot], dst_ref=outbox.at[mine], send_sem=send2.at[k],
            recv_sem=recv2.at[mine], device_id=to(slot), device_id_type=mesh_id,
        )

    def second_wait(piece):
        pltpu.make_async_remote_copy(
            src_ref=result.at[0], dst_ref=outbox.at[piece], send_sem=send2.at[0],
            recv_sem=recv2.at[piece], device_id=to(piece * stride), device_id_type=mesh_id,
        ).wait_recv()

    for k in range(1, pieces):
        first_copy(k).start()
    for_others(lambda: first_copy(0).start())

    def own():
        inbox[me] = drift[mine]
        for k in range(1, n):
            slot = lax.rem(me + k, n)
            pltpu.make_async_remote_copy(
                src_ref=drift.at[mine], dst_ref=inbox.at[slot], send_sem=send1.at[0],
                recv_sem=recv1.at[slot], device_id=to(slot), device_id_type=mesh_id,
            ).wait_recv()
        running = start[mine]
        for j in range(n):
            result[j, 0] = running
            running = running + inbox[j]
        for j in range(n):
            result[j, 1] = running
        for k in range(1, n):
            second_copy(k).start()
        outbox[mine] = result[me]

    for_owner(own)
    for k in range(1, pieces):
        second_wait(lax.rem(mine + k, pieces))

    def rest():
        second_wait(mine)
        first_copy(0).wait_send()

    for_others(rest)
    result_out[...] = outbox[...]
    for k in range(1, pieces):
        first_copy(k).wait_send()

    def sent():
        for k in range(1, n):
            second_copy(k).wait_send()

    for_owner(sent)


def split_kernel(both, new_out, final_out):
    new_out[...] = both[:, 0]
    final_out[...] = both[:, 1]


VMEM = pl.BlockSpec(memory_space=pltpu.VMEM)
SMEM = pl.BlockSpec(memory_space=pltpu.SMEM)
ANY = pl.BlockSpec(memory_space=pl.ANY)


def like(array):
    return pltpu.VMEM(array.shape, array.dtype)


def local(
    timesteps, prompt_ids, start_latent, iterate, fresh_noise, token_table, empty_text, time_in,
    time_out, text_proj, conv_first, spatial_weights, temporal_weights, conv_last,
):
    n = lax.axis_size("slot")
    lat, frames, rows, cols = iterate.shape[1:]
    sections, _, channels, _ = spatial_weights.shape
    width = frames * cols
    pieces = lat * frames
    piece = (rows, cols)
    time_out, text_proj = time_out.T, text_proj.T
    conv_first = conv_first.transpose(0, 2, 1)
    sample = [
        pltpu.VMEM((rows, channels, width), BF16),
        pltpu.VMEM((rows * PAD, width), BF16),
        pltpu.VMEM((PAD, rows * width), BF16),
    ]
    big = [token_table, time_in, time_out, text_proj, spatial_weights, temporal_weights]
    both = pl.pallas_call(
        functools.partial(sweep_kernel, n),
        out_shape=jax.ShapeDtypeStruct((pieces, 2) + piece, F32),
        in_specs=[SMEM] * 2 + [VMEM] * 6 + [ANY] * 6,
        out_specs=VMEM,
        scratch_shapes=[like(w) for w in big]
        + [
            pltpu.SemaphoreType.DMA((4 + 2 * sections,)),
            pltpu.VMEM((sections, channels, 3 * PAD), BF16),
            pltpu.VMEM((sections, channels, PAD), BF16),
            pltpu.VMEM((56, width), F32),
        ]
        + sample * 2
        + [
            pltpu.VMEM((1, token_table.shape[1]), F32),
            pltpu.VMEM((n, 1, token_table.shape[1]), F32),
            pltpu.VMEM((pieces,) + piece, F32),
            pltpu.VMEM((n,) + piece, F32),
            pltpu.VMEM((n, 2) + piece, F32),
            pltpu.VMEM((pieces, 2) + piece, F32),
            pltpu.SemaphoreType.DMA((n,)),
            pltpu.SemaphoreType.DMA((n,)),
            pltpu.SemaphoreType.DMA((pieces,)),
            pltpu.SemaphoreType.DMA((n,)),
            pltpu.SemaphoreType.DMA((n,)),
            pltpu.SemaphoreType.DMA((pieces,)),
        ],
        compiler_params=pltpu.CompilerParams(
            collective_id=0, has_side_effects=True, vmem_limit_bytes=56 * 1024 * 1024
        ),
        cost_estimate=pl.CostEstimate(
            flops=8_000_000_000, bytes_accessed=14_000_000, transcendentals=3_300_000
        ),
        name="sweep",
    )(
        prompt_ids, timesteps, empty_text[None], start_latent.reshape((pieces,) + piece), iterate,
        fresh_noise, conv_first, conv_last, *big,
    )
    shape = jax.ShapeDtypeStruct((pieces,) + piece, F32)
    new, final = pl.pallas_call(
        split_kernel, out_shape=(shape, shape), in_specs=[VMEM], out_specs=(VMEM, VMEM), name="split"
    )(both)
    return new.reshape(iterate.shape), final.reshape(start_latent.shape)


def solution(mesh):
    placed = (
        P(("groups", "slot")),
        P("groups"),
        P("groups", None, None, None),
        P(("groups", "slot"), None, None, None, None),
        P(("groups", "slot"), None, None, None, None),
        P("slot", None),
    ) + (P(),) * 8
    return jax.shard_map(
        local,
        mesh=mesh,
        in_specs=placed,
        out_specs=(P(("groups", "slot"), None, None, None, None), P("groups", None, None, None)),
        check_vma=False,
    )
```

```python
import functools

import jax
import jax.numpy as jnp
import numpy as np
from jax import lax
from jax.experimental import pallas as pl
from jax.experimental.pallas import tpu as pltpu
from jax.sharding import PartitionSpec as P

GROUPS = 32
DT = 50
NORM_EPS = 1e-05
GUIDANCE_SCALE = 5.0
LANES = 128
PAD = 1024
F32 = jnp.float32
BF16 = jnp.bfloat16
LEAD = 3
EARLY = 2


def alpha_bar(step_value):
    phase_angle = (step_value / 1000.0 + 0.008) / 1.008 * (jnp.pi / 2.0)
    cosine = jnp.cos(phase_angle)
    return cosine * cosine


def layer_norm(values):
    average = jnp.mean(values, axis=-1, keepdims=True)
    spread = jnp.mean((values - average) ** 2, axis=-1, keepdims=True)
    return (values - average) * lax.rsqrt(spread + NORM_EPS)


def silu(values):
    half = 0.5 * values
    return half + half * jnp.tanh(half)


def dot(a, b):
    return jnp.dot(a, b, preferred_element_type=F32)


def shift(tile, step):
    if step == 0:
        return tile
    lane = lax.broadcasted_iota(jnp.int32, tile.shape, 1)
    rolled = pltpu.roll(tile, (-step) % LANES, axis=1)
    return jnp.where(lane == (LANES - 1 if step == 1 else 0), 0.0, rolled)


def group_matrix(channels, copies):
    size = channels // GROUPS
    group = lax.broadcasted_iota(jnp.int32, (GROUPS, channels), 0) * size
    channel = lax.broadcasted_iota(jnp.int32, (GROUPS, channels), 1)
    one = jnp.where((channel >= group) & (channel < group + size), 1.0, 0.0)
    return jnp.concatenate([one] * copies, axis=1).astype(BF16)


def expand_matrix(channels):
    size = channels // GROUPS
    channel = lax.broadcasted_iota(jnp.int32, (channels, 3 * GROUPS), 0)
    group = (lax.broadcasted_iota(jnp.int32, (channels, 3 * GROUPS), 1) & (GROUPS - 1)) * size
    return jnp.where((channel >= group) & (channel < group + size), 1.0, 0.0).astype(BF16)


def spread_groups(expand, stat):
    high = stat.astype(BF16)
    rest = stat - high.astype(F32)
    middle = rest.astype(BF16)
    low = (rest - middle.astype(F32)).astype(BF16)
    return dot(expand, jnp.concatenate([high, middle, low], axis=0))


def lane_means(sums, frames, count, temporal):
    tiles = [sums[:, f * LANES : (f + 1) * LANES] for f in range(frames)]
    if temporal:
        tiles = [sum(tiles)]
        count = count * frames
    means = [jnp.sum(tile, axis=1, keepdims=True) * (1.0 / count) for tile in tiles]
    return jnp.concatenate([jnp.broadcast_to(m, (GROUPS, LANES)) for m in means], axis=1)


def norm_silu(state, gather, expand, sizes, temporal):
    _, channels, _, frames, rows = sizes
    count = (channels // GROUPS) * rows * LANES
    values = [state[pl.ds(r * channels, channels), :].astype(F32) for r in range(rows)]
    mean = lane_means(dot(gather, state[...]), frames, count, temporal)
    square = sum(v * v for v in values)
    high = square.astype(BF16)
    low = (square - high.astype(F32)).astype(BF16)
    total = dot(gather, jnp.concatenate([high, low], axis=0))
    spread = jnp.maximum(lane_means(total, frames, count, temporal) - mean * mean, 0.0)
    scale = 0.5 * lax.rsqrt(spread + NORM_EPS)
    both = spread_groups(expand, jnp.concatenate([scale, -mean * scale], axis=1))
    width = scale.shape[1]
    tiles = []
    for r in range(rows):
        tiles.append([])
        for f in range(frames):
            at = 0 if temporal else f * LANES
            half = (
                values[r][:, f * LANES : (f + 1) * LANES] * both[:, at : at + LANES]
                + both[:, width + at : width + at + LANES]
            ).astype(BF16)
            tiles[r].append(half + half * jnp.tanh(half))
    return tiles


def shift_short(tile, step):
    if step == 0:
        return tile
    blank = jnp.zeros((tile.shape[0], 1), tile.dtype)
    if step == 1:
        return jnp.concatenate([tile[:, 1:], blank], axis=1)
    return jnp.concatenate([blank, tile[:, :-1]], axis=1)


def dot_nt(a, b):
    return lax.dot_general(a, b, (((1,), (1,)), ((), ())), preferred_element_type=F32)


def small_taps(weight, rows):
    taps = [weight[k].astype(F32) for k in range(9)]
    lat, channels = taps[0].shape
    return jnp.concatenate(taps + [jnp.zeros((rows - 9 * lat, channels), F32)], axis=0)


def first_windows(latent, first_in):
    lat, frames, rows = latent.shape[1:4]
    first_in[...] = jnp.zeros_like(first_in)
    for r in range(rows):
        for f in range(frames):
            tile = jnp.concatenate([latent[0, l, f, pl.ds(r, 1), :] for l in range(lat)], axis=0)
            for k in range(3):
                first_in[pl.ds((r + 1) * 3 * lat + k * lat, lat), pl.ds(f * LANES, LANES)] = shift(
                    tile, k - 1
                )


def sample_steps(emb, weight, first_in, wcat, wt, w_last, scratch, consts, sizes, predicted, ready):
    state, xs, xt = scratch
    gather, expand = consts
    sections, channels, lat, frames, rows = sizes
    column = jnp.broadcast_to(emb, (LANES, channels)).T
    column = jnp.concatenate([column] * frames, axis=1)
    for r in range(rows):
        window = first_in[pl.ds(r * 3 * lat, weight.shape[1]), :].astype(BF16)
        state[pl.ds(r * channels, channels), :] = (dot(weight, window) + column).astype(BF16)
    yield
    for s in range(sections):
        normed = norm_silu(state, gather, expand, sizes, False)
        for r in range(rows):
            for f in range(frames):
                at = pl.ds(f * LANES, LANES)
                for k in range(3):
                    xs[pl.ds(r * PAD + k * channels, channels), at] = shift_short(
                        normed[r][f], k - 1
                    )
        yield
        ready("spatial", s)
        for r in range(rows):
            moved = dot(wcat[s, :, pl.ds((1 - r) * PAD, 2 * PAD)], xs[...])
            at = pl.ds(r * channels, channels)
            state[at, :] = (state[at, :].astype(F32) + moved).astype(BF16)
        yield
        normed = norm_silu(state, gather, expand, sizes, True)
        for r in range(rows):
            for f in range(frames):
                for k in range(3):
                    to = f - (k - 1)
                    if 0 <= to < frames:
                        xt[pl.ds(k * channels, channels), pl.ds((r * frames + to) * LANES, LANES)] = normed[r][f]
        yield
        ready("temporal", s)
        for r in range(rows):
            moved = dot(wt[s], xt[:, pl.ds(r * frames * LANES, frames * LANES)])
            at = pl.ds(r * channels, channels)
            state[at, :] = (state[at, :].astype(F32) + moved).astype(BF16)
        yield
    normed = norm_silu(state, gather, expand, sizes, False)
    yield
    ready("last")
    taps_last = small_taps(w_last, 48).astype(BF16)
    taps = [dot(taps_last, jnp.concatenate(normed[r], axis=1)) for r in range(rows)]
    for r in range(rows):
        for f in range(frames):
            total = None
            for k in range(3):
                tile = sum(
                    taps[q][((q - r + 1) * 3 + k) * lat :][:lat, f * LANES : (f + 1) * LANES]
                    for q in range(rows)
                )
                term = shift(tile, k - 1)
                total = term if total is None else total + term
            predicted[r][f] = total
    yield


def text_row(row, text_proj):
    pair = layer_norm(row).astype(BF16)
    return dot_nt(jnp.broadcast_to(pair, (16, row.shape[1])), text_proj[...])[0:1]


def time_row(timesteps, time_in, time_out, ready):
    channels = time_in.shape[0]
    half = channels // 2
    lane = lax.broadcasted_iota(jnp.int32, (16, channels), 1)
    place = jnp.where(lane < half, lane, lane - half).astype(F32)
    step = jnp.full((16, channels), timesteps[0], jnp.int32).astype(F32)
    angles = step * jnp.exp(np.float32(-np.log(10000.0)) * place / half)
    feature = jnp.where(lane < half, jnp.cos(angles), jnp.sin(angles)).astype(BF16)
    ready("time_in")
    hidden = silu(dot(feature, time_in[...])).astype(BF16)
    ready("time_out")
    return dot_nt(hidden, time_out[...])[0:1]


def drift_factors(timesteps):
    step_value = jnp.full((8, LANES), timesteps[0], jnp.int32).astype(F32)
    now = alpha_bar(step_value)
    prev = alpha_bar(step_value - DT)
    ratio = jnp.sqrt(prev / now)
    noise_square = (1.0 - prev) * (1.0 - now / prev) / (1.0 - now)
    kept_square = (1.0 - prev) * (now / prev - now) / (1.0 - now)
    eps_factor = (jnp.sqrt(kept_square) - ratio * jnp.sqrt(1.0 - now))[0:1]
    return (ratio - 1.0)[0:1], eps_factor, jnp.sqrt(noise_square)[0:1]


def token_counts(prompt, shard_rows, me):
    amount = prompt.shape[0]
    base = me * shard_rows
    sub = lax.broadcasted_iota(jnp.int32, (16, LANES), 0)
    wide = -(-shard_rows // LANES) * LANES
    lane = lax.broadcasted_iota(jnp.int32, (16, wide), 1)
    counts = jnp.zeros((16, wide), F32)
    for start in range(0, amount, 16):
        column = jnp.full((16, LANES), -1, jnp.int32)
        for j in range(min(16, amount - start)):
            column = jnp.where(sub == j, prompt[start + j] - base, column)
        column = jnp.concatenate([column] * (wide // LANES), axis=1)
        counts = counts + jnp.where(lane == column, 1.0, 0.0)
    return counts[:, :shard_rows].astype(BF16)


def sweep_kernel(
    n, prompt, timesteps, empty, start, latent, fresh, first, last, table_hbm, time_in_hbm,
    time_out_hbm, text_hbm, spatial_hbm, temporal_hbm, result_out,
    table, time_in, time_out, text_proj, spatial, temporal, sem,
    wcat, wt, first_in, state_u, xs_u, xt_u, state_c, xs_c, xt_c,
    partial, pool, drift, inbox, result, outbox, sendp, recvp, send1, recv1, send2, recv2,
):
    mesh_id = pl.DeviceIdType.MESH
    sections, _, channels, _ = spatial.shape
    lat, frames, rows = latent.shape[1:4]
    me = lax.axis_index("slot")
    barrier = pltpu.get_barrier_semaphore()

    def to(slot):
        return {"slot": slot}

    copies = {}
    names = [
        (("time_in",), time_in_hbm, time_in),
        (("time_out",), time_out_hbm, time_out),
        (("text",), text_hbm, text_proj),
        (("table",), table_hbm, table),
    ]
    for s in range(sections):
        names.append((("spatial", s), spatial_hbm.at[s], spatial.at[s]))
        names.append((("temporal", s), temporal_hbm.at[s], temporal.at[s]))
    for index, (key, source, target) in enumerate(names):
        copies[key] = pltpu.make_async_copy(source, target, sem.at[index])
        copies[key].start()
    for k in range(1, n):
        pl.semaphore_signal(barrier, inc=1, device_id=to(lax.rem(me + k, n)), device_id_type=mesh_id)

    done = set()
    blank = jnp.zeros((channels, PAD - 3 * channels), BF16)

    def ready(*key):
        if key in done:
            return
        done.add(key)
        if key in copies:
            copies[key].wait()
        if key[0] == "spatial":
            s = key[1]
            for g in range(3):
                wcat[s, :, pl.ds(g * PAD, PAD)] = jnp.concatenate(
                    [spatial[s, 3 * g + k] for k in range(3)] + [blank], axis=1
                )
        if key[0] == "temporal":
            s = key[1]
            wt[s] = jnp.concatenate([temporal[s, k] for k in range(3)] + [blank], axis=1)

    for ref in (xs_u, xs_c):
        for r in range(rows):
            ref[pl.ds(r * PAD + 3 * channels, PAD - 3 * channels), :] = jnp.zeros(
                (PAD - 3 * channels, ref.shape[1]), BF16
            )
    for ref in (xt_u, xt_c):
        ref[...] = jnp.zeros_like(ref)
    counts = token_counts(prompt, table.shape[0], me)
    first_windows(latent, first_in)
    weight = small_taps(first, 40).T.astype(BF16)
    consts = (group_matrix(channels, rows), expand_matrix(channels))
    sizes = (sections, channels, lat, frames, rows)
    keep, eps_factor, noise_factor = drift_factors(timesteps)
    tvec = time_row(timesteps, time_in, time_out, ready)
    ready("text")
    emb_u = tvec + text_row(empty[...], text_proj)

    pred_u = [[None] * frames for _ in range(rows)]
    pred_c = [[None] * frames for _ in range(rows)]
    steps_u = sample_steps(
        emb_u, weight, first_in, wcat, wt, last, (state_u, xs_u, xt_u), consts, sizes, pred_u, ready
    )
    for _ in range(EARLY):
        next(steps_u)

    ready("table")
    partial[...] = jnp.sum(dot(counts, table[...]), axis=0, keepdims=True)
    pl.semaphore_wait(barrier, n - 1)

    def pooled_copy(k):
        return pltpu.make_async_remote_copy(
            src_ref=partial, dst_ref=pool.at[me], send_sem=sendp.at[k], recv_sem=recvp.at[me],
            device_id=to(lax.rem(me + k, n)), device_id_type=mesh_id,
        )

    for k in range(1, n):
        pooled_copy(k).start()
    pool[me] = partial[...]

    for _ in range(LEAD - EARLY):
        next(steps_u)

    for s in range(sections):
        ready("spatial", s)
        ready("temporal", s)
    for k in range(1, n):
        slot = lax.rem(me + k, n)
        pltpu.make_async_remote_copy(
            src_ref=partial, dst_ref=pool.at[slot], send_sem=sendp.at[0], recv_sem=recvp.at[slot],
            device_id=to(slot), device_id_type=mesh_id,
        ).wait_recv()
    pooled = pool[0]
    for k in range(1, n):
        pooled = pooled + pool[k]
    emb_c = tvec + text_row(pooled * (1.0 / prompt.shape[0]), text_proj)
    steps_c = sample_steps(
        emb_c, weight, first_in, wcat, wt, last, (state_c, xs_c, xt_c), consts, sizes, pred_c, ready
    )
    live = True
    while live:
        live = next(steps_c, 0) is None
        next(steps_u, 0)

    for r in range(rows):
        for f in range(frames):
            without = pred_u[r][f]
            guided = without + GUIDANCE_SCALE * (pred_c[r][f] - without)
            for l in range(lat):
                drift[l * frames + f, pl.ds(r, 1), :] = (
                    keep * latent[0, l, f, pl.ds(r, 1), :]
                    + eps_factor * guided[l : l + 1]
                    + noise_factor * fresh[0, l, f, pl.ds(r, 1), :]
                )
    exchange(
        n, me, to, drift, start, result_out, inbox, result, outbox, send1, recv1, send2, recv2
    )
    for k in range(1, n):
        pooled_copy(k).wait_send()


def exchange(
    n, me, to, drift, start, result_out, inbox, result, outbox, send1, recv1, send2, recv2
):
    pieces = drift.shape[0]
    stride = n // pieces
    mine = me // stride if stride > 1 else me
    mesh_id = pl.DeviceIdType.MESH

    def for_owner(body):
        pl.when(lax.rem(me, stride) == 0)(body) if stride > 1 else body()

    def for_others(body):
        if stride > 1:
            pl.when(lax.rem(me, stride) != 0)(body)

    def first_copy(k):
        piece = lax.rem(mine + k, pieces)
        return pltpu.make_async_remote_copy(
            src_ref=drift.at[piece], dst_ref=inbox.at[me], send_sem=send1.at[k],
            recv_sem=recv1.at[me], device_id=to(piece * stride), device_id_type=mesh_id,
        )

    def second_copy(k):
        slot = lax.rem(me + k, n)
        return pltpu.make_async_remote_copy(
            src_ref=result.at[slot], dst_ref=outbox.at[mine], send_sem=send2.at[k],
            recv_sem=recv2.at[mine], device_id=to(slot), device_id_type=mesh_id,
        )

    def second_wait(piece):
        pltpu.make_async_remote_copy(
            src_ref=result.at[0], dst_ref=outbox.at[piece], send_sem=send2.at[0],
            recv_sem=recv2.at[piece], device_id=to(piece * stride), device_id_type=mesh_id,
        ).wait_recv()

    for k in range(1, pieces):
        first_copy(k).start()
    for_others(lambda: first_copy(0).start())

    def own():
        inbox[me] = drift[mine]
        for k in range(1, n):
            slot = lax.rem(me + k, n)
            pltpu.make_async_remote_copy(
                src_ref=drift.at[mine], dst_ref=inbox.at[slot], send_sem=send1.at[0],
                recv_sem=recv1.at[slot], device_id=to(slot), device_id_type=mesh_id,
            ).wait_recv()
        running = start[mine]
        for j in range(n):
            result[j, 0] = running
            running = running + inbox[j]
        for j in range(n):
            result[j, 1] = running
        for k in range(1, n):
            second_copy(k).start()
        outbox[mine] = result[me]

    for_owner(own)
    for k in range(1, pieces):
        second_wait(lax.rem(mine + k, pieces))

    def rest():
        second_wait(mine)
        first_copy(0).wait_send()

    for_others(rest)
    result_out[...] = outbox[...]
    for k in range(1, pieces):
        first_copy(k).wait_send()

    def sent():
        for k in range(1, n):
            second_copy(k).wait_send()

    for_owner(sent)


def split_kernel(both, new_out, final_out):
    new_out[...] = both[:, 0]
    final_out[...] = both[:, 1]


VMEM = pl.BlockSpec(memory_space=pltpu.VMEM)
SMEM = pl.BlockSpec(memory_space=pltpu.SMEM)
ANY = pl.BlockSpec(memory_space=pl.ANY)


def like(array):
    return pltpu.VMEM(array.shape, array.dtype)


def local(
    timesteps, prompt_ids, start_latent, iterate, fresh_noise, token_table, empty_text, time_in,
    time_out, text_proj, conv_first, spatial_weights, temporal_weights, conv_last,
):
    n = lax.axis_size("slot")
    lat, frames, rows, cols = iterate.shape[1:]
    sections, _, channels, _ = spatial_weights.shape
    width = frames * cols
    pieces = lat * frames
    piece = (rows, cols)
    time_out, text_proj = time_out.T, text_proj.T
    conv_first = conv_first.transpose(0, 2, 1)
    sample = [
        pltpu.VMEM((rows * channels, width), BF16),
        pltpu.VMEM((rows * PAD, width), BF16),
        pltpu.VMEM((PAD, rows * width), BF16),
    ]
    big = [token_table, time_in, time_out, text_proj, spatial_weights, temporal_weights]
    both = pl.pallas_call(
        functools.partial(sweep_kernel, n),
        out_shape=jax.ShapeDtypeStruct((pieces, 2) + piece, F32),
        in_specs=[SMEM] * 2 + [VMEM] * 6 + [ANY] * 6,
        out_specs=VMEM,
        scratch_shapes=[like(w) for w in big]
        + [
            pltpu.SemaphoreType.DMA((4 + 2 * sections,)),
            pltpu.VMEM((sections, channels, 3 * PAD), BF16),
            pltpu.VMEM((sections, channels, PAD), BF16),
            pltpu.VMEM((56, width), F32),
        ]
        + sample * 2
        + [
            pltpu.VMEM((1, token_table.shape[1]), F32),
            pltpu.VMEM((n, 1, token_table.shape[1]), F32),
            pltpu.VMEM((pieces,) + piece, F32),
            pltpu.VMEM((n,) + piece, F32),
            pltpu.VMEM((n, 2) + piece, F32),
            pltpu.VMEM((pieces, 2) + piece, F32),
            pltpu.SemaphoreType.DMA((n,)),
            pltpu.SemaphoreType.DMA((n,)),
            pltpu.SemaphoreType.DMA((pieces,)),
            pltpu.SemaphoreType.DMA((n,)),
            pltpu.SemaphoreType.DMA((n,)),
            pltpu.SemaphoreType.DMA((pieces,)),
        ],
        compiler_params=pltpu.CompilerParams(
            collective_id=0, has_side_effects=True, vmem_limit_bytes=56 * 1024 * 1024
        ),
        cost_estimate=pl.CostEstimate(
            flops=8_000_000_000, bytes_accessed=14_000_000, transcendentals=3_300_000
        ),
        name="sweep",
    )(
        prompt_ids, timesteps, empty_text[None], start_latent.reshape((pieces,) + piece), iterate,
        fresh_noise, conv_first, conv_last, *big,
    )
    shape = jax.ShapeDtypeStruct((pieces,) + piece, F32)
    new, final = pl.pallas_call(
        split_kernel, out_shape=(shape, shape), in_specs=[VMEM], out_specs=(VMEM, VMEM), name="split"
    )(both)
    return new.reshape(iterate.shape), final.reshape(start_latent.shape)


def solution(mesh):
    placed = (
        P(("groups", "slot")),
        P("groups"),
        P("groups", None, None, None),
        P(("groups", "slot"), None, None, None, None),
        P(("groups", "slot"), None, None, None, None),
        P("slot", None),
    ) + (P(),) * 8
    return jax.shard_map(
        local,
        mesh=mesh,
        in_specs=placed,
        out_specs=(P(("groups", "slot"), None, None, None, None), P("groups", None, None, None)),
        check_vma=False,
    )
```

```python
import functools

import jax
import jax.numpy as jnp
import numpy as np
from jax import lax
from jax.experimental import pallas as pl
from jax.experimental.pallas import tpu as pltpu
from jax.sharding import PartitionSpec as P

GROUPS = 32
DT = 50
NORM_EPS = 1e-05
GUIDANCE_SCALE = 5.0
LANES = 128
PAD = 1024
F32 = jnp.float32
BF16 = jnp.bfloat16
LEAD = 6
EARLY = 4


def alpha_bar(step_value):
    phase_angle = (step_value / 1000.0 + 0.008) / 1.008 * (jnp.pi / 2.0)
    cosine = jnp.cos(phase_angle)
    return cosine * cosine


def layer_norm(values):
    average = jnp.mean(values, axis=-1, keepdims=True)
    spread = jnp.mean((values - average) ** 2, axis=-1, keepdims=True)
    return (values - average) * lax.rsqrt(spread + NORM_EPS)


def silu(values):
    half = 0.5 * values
    return half + half * jnp.tanh(half)


def dot(a, b):
    return jnp.dot(a, b, preferred_element_type=F32)


def shift(tile, step):
    if step == 0:
        return tile
    lane = lax.broadcasted_iota(jnp.int32, tile.shape, 1)
    rolled = pltpu.roll(tile, (-step) % LANES, axis=1)
    return jnp.where(lane == (LANES - 1 if step == 1 else 0), 0.0, rolled)


def group_matrix(channels, copies):
    size = channels // GROUPS
    group = lax.broadcasted_iota(jnp.int32, (GROUPS, channels), 0) * size
    channel = lax.broadcasted_iota(jnp.int32, (GROUPS, channels), 1)
    one = jnp.where((channel >= group) & (channel < group + size), 1.0, 0.0)
    return jnp.concatenate([one] * copies, axis=1).astype(BF16)


def expand_matrix(channels):
    size = channels // GROUPS
    channel = lax.broadcasted_iota(jnp.int32, (channels, 3 * GROUPS), 0)
    group = (lax.broadcasted_iota(jnp.int32, (channels, 3 * GROUPS), 1) & (GROUPS - 1)) * size
    return jnp.where((channel >= group) & (channel < group + size), 1.0, 0.0).astype(BF16)


def spread_groups(expand, stat):
    high = stat.astype(BF16)
    rest = stat - high.astype(F32)
    middle = rest.astype(BF16)
    low = (rest - middle.astype(F32)).astype(BF16)
    return dot(expand, jnp.concatenate([high, middle, low], axis=0))


def lane_means(sums, frames, count):
    means = [
        jnp.sum(sums[:, f * LANES : (f + 1) * LANES], axis=1, keepdims=True) * (1.0 / count)
        for f in range(frames)
    ]
    return jnp.concatenate([jnp.broadcast_to(m, (GROUPS, LANES)) for m in means], axis=1)


def split_terms(value):
    high = value.astype(BF16)
    low = (value - high.astype(F32)).astype(BF16)
    return jnp.concatenate([high, low], axis=0)


def norm_factors(state, gather, expand, sizes, temporal):
    _, channels, _, frames, rows = sizes
    count = (channels // GROUPS) * rows * LANES
    values = [state[pl.ds(r * channels, channels), :].astype(F32) for r in range(rows)]
    square = sum(v * v for v in values)
    if temporal:
        plain = sum(values)
        both = [
            split_terms(sum(v[:, f * LANES : (f + 1) * LANES] for f in range(frames)))
            for v in (plain, square)
        ]
        total = dot(gather, jnp.concatenate(both, axis=1))
        mean = lane_means(total[:, :LANES], 1, count * frames)
        power = lane_means(total[:, LANES:], 1, count * frames)
    else:
        mean = lane_means(dot(gather, state[...]), frames, count)
        power = lane_means(dot(gather, split_terms(square)), frames, count)
    spread = jnp.maximum(power - mean * mean, 0.0)
    scale = 0.5 * lax.rsqrt(spread + NORM_EPS)
    both = spread_groups(expand, jnp.concatenate([scale, -mean * scale], axis=1))
    width = scale.shape[1]
    return both[:, :width], both[:, width:]


def norm_tile(state, factors, sizes, r, f):
    channels = sizes[1]
    scale, bias = factors
    at = f * LANES if scale.shape[1] > LANES else 0
    value = state[pl.ds(r * channels, channels), pl.ds(f * LANES, LANES)].astype(F32)
    half = (value * scale[:, at : at + LANES] + bias[:, at : at + LANES]).astype(BF16)
    return half + half * jnp.tanh(half)


def shift_short(tile, step):
    if step == 0:
        return tile
    blank = jnp.zeros((tile.shape[0], 1), tile.dtype)
    if step == 1:
        return jnp.concatenate([tile[:, 1:], blank], axis=1)
    return jnp.concatenate([blank, tile[:, :-1]], axis=1)


def dot_nt(a, b):
    return lax.dot_general(a, b, (((1,), (1,)), ((), ())), preferred_element_type=F32)


def small_taps(weight, rows):
    taps = [weight[k].astype(F32) for k in range(9)]
    lat, channels = taps[0].shape
    return jnp.concatenate(taps + [jnp.zeros((rows - 9 * lat, channels), F32)], axis=0)


def first_windows(latent, first_in):
    lat, frames, rows = latent.shape[1:4]
    first_in[...] = jnp.zeros_like(first_in)
    for r in range(rows):
        for f in range(frames):
            tile = jnp.concatenate([latent[0, l, f, pl.ds(r, 1), :] for l in range(lat)], axis=0)
            for k in range(3):
                first_in[pl.ds((r + 1) * 3 * lat + k * lat, lat), pl.ds(f * LANES, LANES)] = shift(
                    tile, k - 1
                )


def sample_steps(emb, weight, first_in, wcat, wt, w_last, scratch, consts, sizes, predicted, ready):
    state, xs, xt = scratch
    gather, expand = consts
    sections, channels, lat, frames, rows = sizes
    column = jnp.broadcast_to(emb, (LANES, channels)).T
    column = jnp.concatenate([column] * frames, axis=1)
    for r in range(rows):
        window = first_in[pl.ds(r * 3 * lat, weight.shape[1]), :].astype(BF16)
        state[pl.ds(r * channels, channels), :] = (dot(weight, window) + column).astype(BF16)
    yield
    yield
    half = frames // 2
    width = half * LANES
    for s in range(sections):
        factors = norm_factors(state, gather, expand, sizes, False)
        yield
        for r in range(rows):
            for f in range(frames):
                at = pl.ds(f * LANES, LANES)
                tile = norm_tile(state, factors, sizes, r, f)
                for k in range(3):
                    xs[pl.ds(r * PAD + k * channels, channels), at] = shift_short(tile, k - 1)
        yield
        ready("spatial", s)
        for part in range(2):
            at = pl.ds(part * width, width)
            moved = dot(wcat[s], xs[:, at])
            state[:, at] = (state[:, at].astype(F32) + moved).astype(BF16)
            yield
        factors = norm_factors(state, gather, expand, sizes, True)
        yield
        for r in range(rows):
            for f in range(frames):
                tile = norm_tile(state, factors, sizes, r, f)
                for k in range(3):
                    to = f - (k - 1)
                    if 0 <= to < frames:
                        at = pl.ds((r * frames + to) * LANES, LANES)
                        xt[pl.ds(k * channels, channels), at] = tile
        yield
        ready("temporal", s)
        for r in range(rows):
            moved = dot(wt[s], xt[:, pl.ds(r * frames * LANES, frames * LANES)])
            at = pl.ds(r * channels, channels)
            state[at, :] = (state[at, :].astype(F32) + moved).astype(BF16)
            yield
    factors = norm_factors(state, gather, expand, sizes, False)
    yield
    normed = [[norm_tile(state, factors, sizes, r, f) for f in range(frames)] for r in range(rows)]
    yield
    ready("last")
    taps_last = small_taps(w_last, 48).astype(BF16)
    taps = [dot(taps_last, jnp.concatenate(normed[r], axis=1)) for r in range(rows)]
    for r in range(rows):
        for f in range(frames):
            total = None
            for k in range(3):
                tile = sum(
                    taps[q][((q - r + 1) * 3 + k) * lat :][:lat, f * LANES : (f + 1) * LANES]
                    for q in range(rows)
                )
                term = shift(tile, k - 1)
                total = term if total is None else total + term
            predicted[r][f] = total
    yield


def text_row(row, text_proj):
    pair = layer_norm(row).astype(BF16)
    return dot_nt(jnp.broadcast_to(pair, (16, row.shape[1])), text_proj[...])[0:1]


def time_row(timesteps, time_in, time_out, ready):
    channels = time_in.shape[0]
    half = channels // 2
    lane = lax.broadcasted_iota(jnp.int32, (16, channels), 1)
    place = jnp.where(lane < half, lane, lane - half).astype(F32)
    step = jnp.full((16, channels), timesteps[0], jnp.int32).astype(F32)
    angles = step * jnp.exp(np.float32(-np.log(10000.0)) * place / half)
    feature = jnp.where(lane < half, jnp.cos(angles), jnp.sin(angles)).astype(BF16)
    ready("time_in")
    hidden = silu(dot(feature, time_in[...])).astype(BF16)
    ready("time_out")
    return dot_nt(hidden, time_out[...])[0:1]


def drift_factors(timesteps):
    step_value = jnp.full((8, LANES), timesteps[0], jnp.int32).astype(F32)
    now = alpha_bar(step_value)
    prev = alpha_bar(step_value - DT)
    ratio = jnp.sqrt(prev / now)
    noise_square = (1.0 - prev) * (1.0 - now / prev) / (1.0 - now)
    kept_square = (1.0 - prev) * (now / prev - now) / (1.0 - now)
    eps_factor = (jnp.sqrt(kept_square) - ratio * jnp.sqrt(1.0 - now))[0:1]
    return (ratio - 1.0)[0:1], eps_factor, jnp.sqrt(noise_square)[0:1]


def token_counts(prompt, shard_rows, me):
    amount = prompt.shape[0]
    base = me * shard_rows
    sub = lax.broadcasted_iota(jnp.int32, (16, LANES), 0)
    wide = -(-shard_rows // LANES) * LANES
    lane = lax.broadcasted_iota(jnp.int32, (16, wide), 1)
    counts = jnp.zeros((16, wide), F32)
    for start in range(0, amount, 16):
        column = jnp.full((16, LANES), -1, jnp.int32)
        for j in range(min(16, amount - start)):
            column = jnp.where(sub == j, prompt[start + j] - base, column)
        column = jnp.concatenate([column] * (wide // LANES), axis=1)
        counts = counts + jnp.where(lane == column, 1.0, 0.0)
    return counts[:, :shard_rows].astype(BF16)


def sweep_kernel(
    n, prompt, timesteps, empty, start, latent, fresh, first, last, table_hbm, time_in_hbm,
    time_out_hbm, text_hbm, spatial_hbm, temporal_hbm, result_out,
    table, time_in, time_out, text_proj, spatial, temporal, sem,
    wcat, wt, first_in, state_u, xs_u, xt_u, state_c, xs_c, xt_c,
    partial, pool, drift, inbox, result, outbox, sendp, recvp, send1, recv1, send2, recv2,
):
    mesh_id = pl.DeviceIdType.MESH
    sections, _, channels, _ = spatial.shape
    lat, frames, rows = latent.shape[1:4]
    me = lax.axis_index("slot")
    barrier = pltpu.get_barrier_semaphore()

    def to(slot):
        return {"slot": slot}

    copies = {}
    names = [
        (("time_in",), time_in_hbm, time_in),
        (("time_out",), time_out_hbm, time_out),
        (("text",), text_hbm, text_proj),
        (("table",), table_hbm, table),
    ]
    for s in range(sections):
        names.append((("spatial", s), spatial_hbm.at[s], spatial.at[s]))
        names.append((("temporal", s), temporal_hbm.at[s], temporal.at[s]))
    for index, (key, source, target) in enumerate(names):
        copies[key] = pltpu.make_async_copy(source, target, sem.at[index])
        copies[key].start()
    for k in range(1, n):
        pl.semaphore_signal(barrier, inc=1, device_id=to(lax.rem(me + k, n)), device_id_type=mesh_id)

    done = set()
    blank = jnp.zeros((channels, PAD - 3 * channels), BF16)

    def ready(*key):
        if key in done:
            return
        done.add(key)
        if key in copies:
            copies[key].wait()
        if key[0] == "spatial":
            s = key[1]
            for g in range(3):
                block = jnp.concatenate(
                    [spatial[s, 3 * g + k] for k in range(3)] + [blank], axis=1
                )
                for r in range(rows):
                    q = r + g - 1
                    if 0 <= q < rows:
                        wcat[s, pl.ds(r * channels, channels), pl.ds(q * PAD, PAD)] = block
        if key[0] == "temporal":
            s = key[1]
            wt[s] = jnp.concatenate([temporal[s, k] for k in range(3)] + [blank], axis=1)

    for ref in (xs_u, xs_c):
        for r in range(rows):
            ref[pl.ds(r * PAD + 3 * channels, PAD - 3 * channels), :] = jnp.zeros(
                (PAD - 3 * channels, ref.shape[1]), BF16
            )
    for ref in (xt_u, xt_c):
        ref[...] = jnp.zeros_like(ref)
    counts = token_counts(prompt, table.shape[0], me)
    first_windows(latent, first_in)
    weight = small_taps(first, 40).T.astype(BF16)
    consts = (group_matrix(channels, rows), expand_matrix(channels))
    sizes = (sections, channels, lat, frames, rows)
    keep, eps_factor, noise_factor = drift_factors(timesteps)
    tvec = time_row(timesteps, time_in, time_out, ready)
    ready("text")
    emb_u = tvec + text_row(empty[...], text_proj)

    pred_u = [[None] * frames for _ in range(rows)]
    pred_c = [[None] * frames for _ in range(rows)]
    steps_u = sample_steps(
        emb_u, weight, first_in, wcat, wt, last, (state_u, xs_u, xt_u), consts, sizes, pred_u, ready
    )
    for _ in range(EARLY):
        next(steps_u)

    ready("table")
    partial[...] = jnp.sum(dot(counts, table[...]), axis=0, keepdims=True)
    pl.semaphore_wait(barrier, n - 1)

    def pooled_copy(k):
        return pltpu.make_async_remote_copy(
            src_ref=partial, dst_ref=pool.at[me], send_sem=sendp.at[k], recv_sem=recvp.at[me],
            device_id=to(lax.rem(me + k, n)), device_id_type=mesh_id,
        )

    for k in range(1, n):
        pooled_copy(k).start()
    pool[me] = partial[...]

    for _ in range(LEAD - EARLY):
        next(steps_u)

    for s in range(sections):
        ready("spatial", s)
        ready("temporal", s)
    for k in range(1, n):
        slot = lax.rem(me + k, n)
        pltpu.make_async_remote_copy(
            src_ref=partial, dst_ref=pool.at[slot], send_sem=sendp.at[0], recv_sem=recvp.at[slot],
            device_id=to(slot), device_id_type=mesh_id,
        ).wait_recv()
    pooled = pool[0]
    for k in range(1, n):
        pooled = pooled + pool[k]
    emb_c = tvec + text_row(pooled * (1.0 / prompt.shape[0]), text_proj)
    steps_c = sample_steps(
        emb_c, weight, first_in, wcat, wt, last, (state_c, xs_c, xt_c), consts, sizes, pred_c, ready
    )
    live = True
    while live:
        live = next(steps_c, 0) is None
        next(steps_u, 0)

    for r in range(rows):
        for f in range(frames):
            without = pred_u[r][f]
            guided = without + GUIDANCE_SCALE * (pred_c[r][f] - without)
            for l in range(lat):
                drift[l * frames + f, pl.ds(r, 1), :] = (
                    keep * latent[0, l, f, pl.ds(r, 1), :]
                    + eps_factor * guided[l : l + 1]
                    + noise_factor * fresh[0, l, f, pl.ds(r, 1), :]
                )
    exchange(
        n, me, to, drift, start, result_out, inbox, result, outbox, send1, recv1, send2, recv2
    )
    for k in range(1, n):
        pooled_copy(k).wait_send()


def exchange(
    n, me, to, drift, start, result_out, inbox, result, outbox, send1, recv1, send2, recv2
):
    pieces = drift.shape[0]
    stride = n // pieces
    mine = me // stride if stride > 1 else me
    mesh_id = pl.DeviceIdType.MESH

    def for_owner(body):
        pl.when(lax.rem(me, stride) == 0)(body) if stride > 1 else body()

    def for_others(body):
        if stride > 1:
            pl.when(lax.rem(me, stride) != 0)(body)

    def first_copy(k):
        piece = lax.rem(mine + k, pieces)
        return pltpu.make_async_remote_copy(
            src_ref=drift.at[piece], dst_ref=inbox.at[me], send_sem=send1.at[k],
            recv_sem=recv1.at[me], device_id=to(piece * stride), device_id_type=mesh_id,
        )

    def second_copy(k):
        slot = lax.rem(me + k, n)
        return pltpu.make_async_remote_copy(
            src_ref=result.at[slot], dst_ref=outbox.at[mine], send_sem=send2.at[k],
            recv_sem=recv2.at[mine], device_id=to(slot), device_id_type=mesh_id,
        )

    def second_wait(piece):
        pltpu.make_async_remote_copy(
            src_ref=result.at[0], dst_ref=outbox.at[piece], send_sem=send2.at[0],
            recv_sem=recv2.at[piece], device_id=to(piece * stride), device_id_type=mesh_id,
        ).wait_recv()

    for k in range(1, pieces):
        first_copy(k).start()
    for_others(lambda: first_copy(0).start())

    def own():
        inbox[me] = drift[mine]
        for k in range(1, n):
            slot = lax.rem(me + k, n)
            pltpu.make_async_remote_copy(
                src_ref=drift.at[mine], dst_ref=inbox.at[slot], send_sem=send1.at[0],
                recv_sem=recv1.at[slot], device_id=to(slot), device_id_type=mesh_id,
            ).wait_recv()
        running = start[mine]
        for j in range(n):
            result[j, 0] = running
            running = running + inbox[j]
        for j in range(n):
            result[j, 1] = running
        for k in range(1, n):
            second_copy(k).start()
        outbox[mine] = result[me]

    for_owner(own)
    for k in range(1, pieces):
        second_wait(lax.rem(mine + k, pieces))

    def rest():
        second_wait(mine)
        first_copy(0).wait_send()

    for_others(rest)
    result_out[...] = outbox[...]
    for k in range(1, pieces):
        first_copy(k).wait_send()

    def sent():
        for k in range(1, n):
            second_copy(k).wait_send()

    for_owner(sent)


def split_kernel(both, new_out, final_out):
    new_out[...] = both[:, 0]
    final_out[...] = both[:, 1]


VMEM = pl.BlockSpec(memory_space=pltpu.VMEM)
SMEM = pl.BlockSpec(memory_space=pltpu.SMEM)
ANY = pl.BlockSpec(memory_space=pl.ANY)


def like(array):
    return pltpu.VMEM(array.shape, array.dtype)


def local(
    timesteps, prompt_ids, start_latent, iterate, fresh_noise, token_table, empty_text, time_in,
    time_out, text_proj, conv_first, spatial_weights, temporal_weights, conv_last,
):
    n = lax.axis_size("slot")
    lat, frames, rows, cols = iterate.shape[1:]
    sections, _, channels, _ = spatial_weights.shape
    width = frames * cols
    pieces = lat * frames
    piece = (rows, cols)
    time_out, text_proj = time_out.T, text_proj.T
    conv_first = conv_first.transpose(0, 2, 1)
    sample = [
        pltpu.VMEM((rows * channels, width), BF16),
        pltpu.VMEM((rows * PAD, width), BF16),
        pltpu.VMEM((PAD, rows * width), BF16),
    ]
    big = [token_table, time_in, time_out, text_proj, spatial_weights, temporal_weights]
    both = pl.pallas_call(
        functools.partial(sweep_kernel, n),
        out_shape=jax.ShapeDtypeStruct((pieces, 2) + piece, F32),
        in_specs=[SMEM] * 2 + [VMEM] * 6 + [ANY] * 6,
        out_specs=VMEM,
        scratch_shapes=[like(w) for w in big]
        + [
            pltpu.SemaphoreType.DMA((4 + 2 * sections,)),
            pltpu.VMEM((sections, rows * channels, rows * PAD), BF16),
            pltpu.VMEM((sections, channels, PAD), BF16),
            pltpu.VMEM((56, width), F32),
        ]
        + sample * 2
        + [
            pltpu.VMEM((1, token_table.shape[1]), F32),
            pltpu.VMEM((n, 1, token_table.shape[1]), F32),
            pltpu.VMEM((pieces,) + piece, F32),
            pltpu.VMEM((n,) + piece, F32),
            pltpu.VMEM((n, 2) + piece, F32),
            pltpu.VMEM((pieces, 2) + piece, F32),
            pltpu.SemaphoreType.DMA((n,)),
            pltpu.SemaphoreType.DMA((n,)),
            pltpu.SemaphoreType.DMA((pieces,)),
            pltpu.SemaphoreType.DMA((n,)),
            pltpu.SemaphoreType.DMA((n,)),
            pltpu.SemaphoreType.DMA((pieces,)),
        ],
        compiler_params=pltpu.CompilerParams(
            collective_id=0, has_side_effects=True, vmem_limit_bytes=56 * 1024 * 1024
        ),
        cost_estimate=pl.CostEstimate(
            flops=8_000_000_000, bytes_accessed=14_000_000, transcendentals=3_300_000
        ),
        name="sweep",
    )(
        prompt_ids, timesteps, empty_text[None], start_latent.reshape((pieces,) + piece), iterate,
        fresh_noise, conv_first, conv_last, *big,
    )
    shape = jax.ShapeDtypeStruct((pieces,) + piece, F32)
    new, final = pl.pallas_call(
        split_kernel, out_shape=(shape, shape), in_specs=[VMEM], out_specs=(VMEM, VMEM), name="split"
    )(both)
    return new.reshape(iterate.shape), final.reshape(start_latent.shape)


def solution(mesh):
    placed = (
        P(("groups", "slot")),
        P("groups"),
        P("groups", None, None, None),
        P(("groups", "slot"), None, None, None, None),
        P(("groups", "slot"), None, None, None, None),
        P("slot", None),
    ) + (P(),) * 8
    return jax.shard_map(
        local,
        mesh=mesh,
        in_specs=placed,
        out_specs=(P(("groups", "slot"), None, None, None, None), P("groups", None, None, None)),
        check_vma=False,
    )
```

```python
import functools

import jax
import jax.numpy as jnp
import numpy as np
from jax import lax
from jax.experimental import pallas as pl
from jax.experimental.pallas import tpu as pltpu
from jax.sharding import PartitionSpec as P

GROUPS = 32
DT = 50
NORM_EPS = 1e-05
GUIDANCE_SCALE = 5.0
LANES = 128
PAD = 1024
F32 = jnp.float32
BF16 = jnp.bfloat16


def alpha_bar(step_value):
    phase_angle = (step_value / 1000.0 + 0.008) / 1.008 * (jnp.pi / 2.0)
    cosine = jnp.cos(phase_angle)
    return cosine * cosine


def layer_norm(values):
    average = jnp.mean(values, axis=-1, keepdims=True)
    spread = jnp.mean((values - average) ** 2, axis=-1, keepdims=True)
    return (values - average) * lax.rsqrt(spread + NORM_EPS)


def silu(values):
    half = 0.5 * values
    return half + half * jnp.tanh(half)


def dot(a, b):
    return jnp.dot(a, b, preferred_element_type=F32)


def shift(tile, step):
    if step == 0:
        return tile
    lane = lax.broadcasted_iota(jnp.int32, tile.shape, 1)
    rolled = pltpu.roll(tile, (-step) % LANES, axis=1)
    return jnp.where(lane == (LANES - 1 if step == 1 else 0), 0.0, rolled)


def group_matrix(channels, copies):
    size = channels // GROUPS
    group = lax.broadcasted_iota(jnp.int32, (GROUPS, channels), 0) * size
    channel = lax.broadcasted_iota(jnp.int32, (GROUPS, channels), 1)
    one = jnp.where((channel >= group) & (channel < group + size), 1.0, 0.0)
    return jnp.concatenate([one] * copies, axis=1).astype(BF16)


def expand_matrix(channels):
    size = channels // GROUPS
    channel = lax.broadcasted_iota(jnp.int32, (channels, 3 * GROUPS), 0)
    group = (lax.broadcasted_iota(jnp.int32, (channels, 3 * GROUPS), 1) & (GROUPS - 1)) * size
    return jnp.where((channel >= group) & (channel < group + size), 1.0, 0.0).astype(BF16)


def spread_groups(expand, stat):
    high = stat.astype(BF16)
    rest = stat - high.astype(F32)
    middle = rest.astype(BF16)
    low = (rest - middle.astype(F32)).astype(BF16)
    return dot(expand, jnp.concatenate([high, middle, low], axis=0))


def lane_means(sums, frames, count):
    means = [
        jnp.sum(sums[:, f * LANES : (f + 1) * LANES], axis=1, keepdims=True) * (1.0 / count)
        for f in range(frames)
    ]
    return jnp.concatenate([jnp.broadcast_to(m, (GROUPS, LANES)) for m in means], axis=1)


def split_terms(value):
    high = value.astype(BF16)
    low = (value - high.astype(F32)).astype(BF16)
    return jnp.concatenate([high, low], axis=0)


def norm_factors(state, gather, expand, sizes, temporal):
    _, channels, _, frames, rows = sizes
    count = (channels // GROUPS) * rows * LANES
    values = [state[pl.ds(r * channels, channels), :].astype(F32) for r in range(rows)]
    square = sum(v * v for v in values)
    if temporal:
        plain = sum(values)
        both = [
            split_terms(sum(v[:, f * LANES : (f + 1) * LANES] for f in range(frames)))
            for v in (plain, square)
        ]
        total = dot(gather, jnp.concatenate(both, axis=1))
        mean = lane_means(total[:, :LANES], 1, count * frames)
        power = lane_means(total[:, LANES:], 1, count * frames)
    else:
        mean = lane_means(dot(gather, state[...]), frames, count)
        power = lane_means(dot(gather, split_terms(square)), frames, count)
    spread = jnp.maximum(power - mean * mean, 0.0)
    scale = 0.5 * lax.rsqrt(spread + NORM_EPS)
    both = spread_groups(expand, jnp.concatenate([scale, -mean * scale], axis=1))
    width = scale.shape[1]
    return both[:, :width], both[:, width:]


def norm_tile(state, factors, sizes, r, f):
    channels = sizes[1]
    scale, bias = factors
    at = f * LANES if scale.shape[1] > LANES else 0
    value = state[pl.ds(r * channels, channels), pl.ds(f * LANES, LANES)].astype(F32)
    half = (value * scale[:, at : at + LANES] + bias[:, at : at + LANES]).astype(BF16)
    return half + half * jnp.tanh(half)


def shift_short(tile, step):
    if step == 0:
        return tile
    blank = jnp.zeros((tile.shape[0], 1), tile.dtype)
    if step == 1:
        return jnp.concatenate([tile[:, 1:], blank], axis=1)
    return jnp.concatenate([blank, tile[:, :-1]], axis=1)


def dot_nt(a, b):
    return lax.dot_general(a, b, (((1,), (1,)), ((), ())), preferred_element_type=F32)


def small_taps(weight, rows):
    taps = [weight[k].astype(F32) for k in range(9)]
    lat, channels = taps[0].shape
    return jnp.concatenate(taps + [jnp.zeros((rows - 9 * lat, channels), F32)], axis=0)


def first_windows(latent, first_in):
    lat, frames, rows = latent.shape[1:4]
    first_in[...] = jnp.zeros_like(first_in)
    for r in range(rows):
        for f in range(frames):
            tile = jnp.concatenate([latent[0, l, f, pl.ds(r, 1), :] for l in range(lat)], axis=0)
            for k in range(3):
                first_in[pl.ds((r + 1) * 3 * lat + k * lat, lat), pl.ds(f * LANES, LANES)] = shift(
                    tile, k - 1
                )


def sample(emb, weight, first_in, wcat, wt, w_last, scratch, consts, sizes, predicted):
    state, xs, xt = scratch
    gather, expand = consts
    sections, channels, lat, frames, rows = sizes
    column = jnp.broadcast_to(emb, (LANES, channels)).T
    column = jnp.concatenate([column] * frames, axis=1)
    for r in range(rows):
        window = first_in[pl.ds(r * 3 * lat, weight.shape[1]), :].astype(BF16)
        state[pl.ds(r * channels, channels), :] = (dot(weight, window) + column).astype(BF16)
    width = frames * LANES

    def section(s, carry):
        factors = norm_factors(state, gather, expand, sizes, False)
        for r in range(rows):
            for f in range(frames):
                at = pl.ds(f * LANES, LANES)
                tile = norm_tile(state, factors, sizes, r, f)
                for k in range(3):
                    xs[pl.ds(r * PAD + k * channels, channels), at] = shift_short(tile, k - 1)
        moved = dot(wcat[s], xs[...])
        state[...] = (state[...].astype(F32) + moved).astype(BF16)
        factors = norm_factors(state, gather, expand, sizes, True)
        for r in range(rows):
            for f in range(frames):
                tile = norm_tile(state, factors, sizes, r, f)
                for k in range(3):
                    to = f - (k - 1)
                    if 0 <= to < frames:
                        at = pl.ds((r * frames + to) * LANES, LANES)
                        xt[pl.ds(k * channels, channels), at] = tile
        for r in range(rows):
            moved = dot(wt[s], xt[:, pl.ds(r * width, width)])
            at = pl.ds(r * channels, channels)
            state[at, :] = (state[at, :].astype(F32) + moved).astype(BF16)
        return carry

    lax.fori_loop(0, sections, section, 0)
    factors = norm_factors(state, gather, expand, sizes, False)
    normed = [[norm_tile(state, factors, sizes, r, f) for f in range(frames)] for r in range(rows)]
    taps_last = small_taps(w_last, 48).astype(BF16)
    taps = [dot(taps_last, jnp.concatenate(normed[r], axis=1)) for r in range(rows)]
    for r in range(rows):
        for f in range(frames):
            total = None
            for k in range(3):
                tile = sum(
                    taps[q][((q - r + 1) * 3 + k) * lat :][:lat, f * LANES : (f + 1) * LANES]
                    for q in range(rows)
                )
                term = shift(tile, k - 1)
                total = term if total is None else total + term
            predicted[r, f] = total


def text_row(row, text_proj):
    pair = layer_norm(row).astype(BF16)
    return dot_nt(jnp.broadcast_to(pair, (16, row.shape[1])), text_proj[...])[0:1]


def time_row(timesteps, time_in, time_out, ready):
    channels = time_in.shape[0]
    half = channels // 2
    lane = lax.broadcasted_iota(jnp.int32, (16, channels), 1)
    place = jnp.where(lane < half, lane, lane - half).astype(F32)
    step = jnp.full((16, channels), timesteps[0], jnp.int32).astype(F32)
    angles = step * jnp.exp(np.float32(-np.log(10000.0)) * place / half)
    feature = jnp.where(lane < half, jnp.cos(angles), jnp.sin(angles)).astype(BF16)
    ready("time_in")
    hidden = silu(dot(feature, time_in[...])).astype(BF16)
    ready("time_out")
    return dot_nt(hidden, time_out[...])[0:1]


def drift_factors(timesteps):
    step_value = jnp.full((8, LANES), timesteps[0], jnp.int32).astype(F32)
    now = alpha_bar(step_value)
    prev = alpha_bar(step_value - DT)
    ratio = jnp.sqrt(prev / now)
    noise_square = (1.0 - prev) * (1.0 - now / prev) / (1.0 - now)
    kept_square = (1.0 - prev) * (now / prev - now) / (1.0 - now)
    eps_factor = (jnp.sqrt(kept_square) - ratio * jnp.sqrt(1.0 - now))[0:1]
    return (ratio - 1.0)[0:1], eps_factor, jnp.sqrt(noise_square)[0:1]


def token_counts(prompt, shard_rows, me):
    amount = prompt.shape[0]
    base = me * shard_rows
    sub = lax.broadcasted_iota(jnp.int32, (16, LANES), 0)
    wide = -(-shard_rows // LANES) * LANES
    lane = lax.broadcasted_iota(jnp.int32, (16, wide), 1)
    counts = jnp.zeros((16, wide), F32)
    for start in range(0, amount, 16):
        column = jnp.full((16, LANES), -1, jnp.int32)
        for j in range(min(16, amount - start)):
            column = jnp.where(sub == j, prompt[start + j] - base, column)
        column = jnp.concatenate([column] * (wide // LANES), axis=1)
        counts = counts + jnp.where(lane == column, 1.0, 0.0)
    return counts[:, :shard_rows].astype(BF16)


def sweep_kernel(
    n, prompt, timesteps, empty, start, latent, fresh, first, last, table_hbm, time_in_hbm,
    time_out_hbm, text_hbm, spatial_hbm, temporal_hbm, result_out,
    table, time_in, time_out, text_proj, spatial, temporal, sem,
    wcat, wt, first_in, state, xs, xt, emb, predicted, weight_ref,
    partial, pool, drift, inbox, result, outbox, sendp, recvp, send1, recv1, send2, recv2,
):
    mesh_id = pl.DeviceIdType.MESH
    sections, _, channels, _ = spatial.shape
    lat, frames, rows = latent.shape[1:4]
    me = lax.axis_index("slot")
    barrier = pltpu.get_barrier_semaphore()

    def to(slot):
        return {"slot": slot}

    copies = {}
    names = [
        (("time_in",), time_in_hbm, time_in),
        (("time_out",), time_out_hbm, time_out),
        (("text",), text_hbm, text_proj),
        (("table",), table_hbm, table),
    ]
    for s in range(sections):
        names.append((("spatial", s), spatial_hbm.at[s], spatial.at[s]))
        names.append((("temporal", s), temporal_hbm.at[s], temporal.at[s]))
    for index, (key, source, target) in enumerate(names):
        copies[key] = pltpu.make_async_copy(source, target, sem.at[index])
        copies[key].start()
    for k in range(1, n):
        pl.semaphore_signal(barrier, inc=1, device_id=to(lax.rem(me + k, n)), device_id_type=mesh_id)

    done = set()
    blank = jnp.zeros((channels, PAD - 3 * channels), BF16)

    def ready(*key):
        if key in done:
            return
        done.add(key)
        if key in copies:
            copies[key].wait()
        if key[0] == "spatial":
            s = key[1]
            for g in range(3):
                block = jnp.concatenate(
                    [spatial[s, 3 * g + k] for k in range(3)] + [blank], axis=1
                )
                for r in range(rows):
                    q = r + g - 1
                    if 0 <= q < rows:
                        wcat[s, pl.ds(r * channels, channels), pl.ds(q * PAD, PAD)] = block
        if key[0] == "temporal":
            s = key[1]
            wt[s] = jnp.concatenate([temporal[s, k] for k in range(3)] + [blank], axis=1)

    for r in range(rows):
        xs[pl.ds(r * PAD + 3 * channels, PAD - 3 * channels), :] = jnp.zeros(
            (PAD - 3 * channels, xs.shape[1]), BF16
        )
    xt[...] = jnp.zeros_like(xt)
    counts = token_counts(prompt, table.shape[0], me)
    first_windows(latent, first_in)
    weight_ref[...] = small_taps(first, 40).T.astype(BF16)
    consts = (group_matrix(channels, rows), expand_matrix(channels))
    sizes = (sections, channels, lat, frames, rows)
    keep, eps_factor, noise_factor = drift_factors(timesteps)
    tvec = time_row(timesteps, time_in, time_out, ready)
    ready("text")
    emb[0] = tvec
    emb[1] = tvec + text_row(empty[...], text_proj)

    ready("table")
    partial[...] = jnp.sum(dot(counts, table[...]), axis=0, keepdims=True)
    pl.semaphore_wait(barrier, n - 1)

    def pooled_copy(k):
        return pltpu.make_async_remote_copy(
            src_ref=partial, dst_ref=pool.at[me], send_sem=sendp.at[k], recv_sem=recvp.at[me],
            device_id=to(lax.rem(me + k, n)), device_id_type=mesh_id,
        )

    for k in range(1, n):
        pooled_copy(k).start()
    pool[me] = partial[...]

    for s in range(sections):
        ready("spatial", s)
        ready("temporal", s)

    def turn(i, carry):
        @pl.when(i == 1)
        def _():
            for k in range(1, n):
                slot = lax.rem(me + k, n)
                pltpu.make_async_remote_copy(
                    src_ref=partial, dst_ref=pool.at[slot], send_sem=sendp.at[0],
                    recv_sem=recvp.at[slot], device_id=to(slot), device_id_type=mesh_id,
                ).wait_recv()
            pooled = pool[0]
            for k in range(1, n):
                pooled = pooled + pool[k]
            emb[0] = emb[0] + text_row(pooled * (1.0 / prompt.shape[0]), text_proj)

        sample(
            emb[1 - i], weight_ref[...], first_in, wcat, wt, last, (state, xs, xt), consts, sizes,
            predicted.at[i],
        )
        return carry

    lax.fori_loop(0, 2, turn, 0)
    for r in range(rows):
        for f in range(frames):
            without = predicted[0, r, f]
            guided = without + GUIDANCE_SCALE * (predicted[1, r, f] - without)
            for l in range(lat):
                drift[l * frames + f, pl.ds(r, 1), :] = (
                    keep * latent[0, l, f, pl.ds(r, 1), :]
                    + eps_factor * guided[l : l + 1]
                    + noise_factor * fresh[0, l, f, pl.ds(r, 1), :]
                )
    exchange(
        n, me, to, drift, start, result_out, inbox, result, outbox, send1, recv1, send2, recv2
    )
    for k in range(1, n):
        pooled_copy(k).wait_send()


def exchange(
    n, me, to, drift, start, result_out, inbox, result, outbox, send1, recv1, send2, recv2
):
    pieces = drift.shape[0]
    stride = n // pieces
    mine = me // stride if stride > 1 else me
    mesh_id = pl.DeviceIdType.MESH

    def for_owner(body):
        pl.when(lax.rem(me, stride) == 0)(body) if stride > 1 else body()

    def for_others(body):
        if stride > 1:
            pl.when(lax.rem(me, stride) != 0)(body)

    def first_copy(k):
        piece = lax.rem(mine + k, pieces)
        return pltpu.make_async_remote_copy(
            src_ref=drift.at[piece], dst_ref=inbox.at[me], send_sem=send1.at[k],
            recv_sem=recv1.at[me], device_id=to(piece * stride), device_id_type=mesh_id,
        )

    def second_copy(k):
        slot = lax.rem(me + k, n)
        return pltpu.make_async_remote_copy(
            src_ref=result.at[slot], dst_ref=outbox.at[mine], send_sem=send2.at[k],
            recv_sem=recv2.at[mine], device_id=to(slot), device_id_type=mesh_id,
        )

    def second_wait(piece):
        pltpu.make_async_remote_copy(
            src_ref=result.at[0], dst_ref=outbox.at[piece], send_sem=send2.at[0],
            recv_sem=recv2.at[piece], device_id=to(piece * stride), device_id_type=mesh_id,
        ).wait_recv()

    for k in range(1, pieces):
        first_copy(k).start()
    for_others(lambda: first_copy(0).start())

    def own():
        inbox[me] = drift[mine]
        for k in range(1, n):
            slot = lax.rem(me + k, n)
            pltpu.make_async_remote_copy(
                src_ref=drift.at[mine], dst_ref=inbox.at[slot], send_sem=send1.at[0],
                recv_sem=recv1.at[slot], device_id=to(slot), device_id_type=mesh_id,
            ).wait_recv()
        running = start[mine]
        for j in range(n):
            result[j, 0] = running
            running = running + inbox[j]
        for j in range(n):
            result[j, 1] = running
        for k in range(1, n):
            second_copy(k).start()
        outbox[mine] = result[me]

    for_owner(own)
    for k in range(1, pieces):
        second_wait(lax.rem(mine + k, pieces))

    def rest():
        second_wait(mine)
        first_copy(0).wait_send()

    for_others(rest)
    result_out[...] = outbox[...]
    for k in range(1, pieces):
        first_copy(k).wait_send()

    def sent():
        for k in range(1, n):
            second_copy(k).wait_send()

    for_owner(sent)


def split_kernel(both, new_out, final_out):
    new_out[...] = both[:, 0]
    final_out[...] = both[:, 1]


VMEM = pl.BlockSpec(memory_space=pltpu.VMEM)
SMEM = pl.BlockSpec(memory_space=pltpu.SMEM)
ANY = pl.BlockSpec(memory_space=pl.ANY)


def like(array):
    return pltpu.VMEM(array.shape, array.dtype)


def local(
    timesteps, prompt_ids, start_latent, iterate, fresh_noise, token_table, empty_text, time_in,
    time_out, text_proj, conv_first, spatial_weights, temporal_weights, conv_last,
):
    n = lax.axis_size("slot")
    lat, frames, rows, cols = iterate.shape[1:]
    sections, _, channels, _ = spatial_weights.shape
    width = frames * cols
    pieces = lat * frames
    piece = (rows, cols)
    time_out, text_proj = time_out.T, text_proj.T
    conv_first = conv_first.transpose(0, 2, 1)
    sample_scratch = [
        pltpu.VMEM((rows * channels, width), BF16),
        pltpu.VMEM((rows * PAD, width), BF16),
        pltpu.VMEM((PAD, rows * width), BF16),
    ]
    big = [token_table, time_in, time_out, text_proj, spatial_weights, temporal_weights]
    both = pl.pallas_call(
        functools.partial(sweep_kernel, n),
        out_shape=jax.ShapeDtypeStruct((pieces, 2) + piece, F32),
        in_specs=[SMEM] * 2 + [VMEM] * 6 + [ANY] * 6,
        out_specs=VMEM,
        scratch_shapes=[like(w) for w in big]
        + [
            pltpu.SemaphoreType.DMA((4 + 2 * sections,)),
            pltpu.VMEM((sections, rows * channels, rows * PAD), BF16),
            pltpu.VMEM((sections, channels, PAD), BF16),
            pltpu.VMEM((56, width), F32),
        ]
        + sample_scratch
        + [
            pltpu.VMEM((2, 1, channels), F32),
            pltpu.VMEM((2, rows, frames, lat, cols), F32),
            pltpu.VMEM((channels, 40), BF16),
            pltpu.VMEM((1, token_table.shape[1]), F32),
            pltpu.VMEM((n, 1, token_table.shape[1]), F32),
            pltpu.VMEM((pieces,) + piece, F32),
            pltpu.VMEM((n,) + piece, F32),
            pltpu.VMEM((n, 2) + piece, F32),
            pltpu.VMEM((pieces, 2) + piece, F32),
            pltpu.SemaphoreType.DMA((n,)),
            pltpu.SemaphoreType.DMA((n,)),
            pltpu.SemaphoreType.DMA((pieces,)),
            pltpu.SemaphoreType.DMA((n,)),
            pltpu.SemaphoreType.DMA((n,)),
            pltpu.SemaphoreType.DMA((pieces,)),
        ],
        compiler_params=pltpu.CompilerParams(
            collective_id=0, has_side_effects=True, vmem_limit_bytes=56 * 1024 * 1024
        ),
        cost_estimate=pl.CostEstimate(
            flops=8_000_000_000, bytes_accessed=14_000_000, transcendentals=3_300_000
        ),
        name="sweep",
    )(
        prompt_ids, timesteps, empty_text[None], start_latent.reshape((pieces,) + piece), iterate,
        fresh_noise, conv_first, conv_last, *big,
    )
    shape = jax.ShapeDtypeStruct((pieces,) + piece, F32)
    new, final = pl.pallas_call(
        split_kernel, out_shape=(shape, shape), in_specs=[VMEM], out_specs=(VMEM, VMEM), name="split"
    )(both)
    return new.reshape(iterate.shape), final.reshape(start_latent.shape)


def solution(mesh):
    placed = (
        P(("groups", "slot")),
        P("groups"),
        P("groups", None, None, None),
        P(("groups", "slot"), None, None, None, None),
        P(("groups", "slot"), None, None, None, None),
        P("slot", None),
    ) + (P(),) * 8
    return jax.shard_map(
        local,
        mesh=mesh,
        in_specs=placed,
        out_specs=(P(("groups", "slot"), None, None, None, None), P("groups", None, None, None)),
        check_vma=False,
    )
```
